512 devices in a mesh: leaf: 64 (over y, z), dom: 2 (over core), rep: 4 (over x).
Axes of the slice: x: 4, y: 4, z: 16, core: 2. Of those that a mesh axis runs over, the one named last changes fastest.
Arguments:
- leaf_basis: bfloat16 [2048, 512, 128], P(('leaf', 'dom', 'rep')), as said below
- transfer: float32 [3584, 128, 128], P(('leaf', 'dom', 'rep')), as said below
- transfer_top: float32 [256, 128, 128], P(('leaf', 'dom')), as said below
- coupling_parts: bfloat16 [4, 8192, 128, 128], P('rep', ('leaf', 'dom')), may hold values from -1 to 1
- row_slot: int32 [8192], P(('leaf', 'dom', 'rep')), may hold values from 0 to 6, as said below
- col_node: int32 [8192], P(('leaf', 'dom', 'rep')), may hold values from 0 to 3583, as said below
Outputs:
- leaf_orth: bfloat16 [2048, 512, 128], P(('leaf', 'dom', 'rep'))
- new_transfer: float32 [3584, 128, 128], P(('leaf', 'dom', 'rep'))
- new_top: float32 [256, 128, 128], P(('leaf', 'dom'), 'rep')
- top_factor: float32 [128, 128, 128], P(('leaf', 'dom'), 'rep')
- coupling_new: bfloat16 [8192, 128, 128], P(('leaf', 'dom', 'rep'))
The draws below stay inside these ranges and needn't reach their ends.
Inputs may be any that keep to these rules, and one draw needn't show every extreme that they name: `leaf_basis`: every leaf block has full column rank. Every transfer factor is invertible. `transfer_top`: every transfer factor is invertible. `row_slot`: slots 0 to 3 are the holding device's four leaves, 4 and 5 its two level-1 nodes, 6 its level-2 node; the holder of block k is device position k // 16 along leaf+dom+rep. col_node[k] = 7 d + c, where d is a device position along leaf+dom+rep at most 2 away from the holder of block k and c is a slot of the same level as row_slot[k] (0 to 3, 4 to 5, or 6); the first block of every device has its column node exactly 2 positions away.
All inputs are finite; a program needn't handle non-finite values.
Results may differ from the reference program's by a relative error of at most 0.013.
Values may be sent and summed in bfloat16 or wider, within the bound.
A program may use at most 64 MiB of HBM per device.

```python
import math
import jax
import jax.numpy as jnp
from jax import lax

RANK = 128
PTS = 512
TILE_DEV = 16
REACH = 2
NLEAF = 2048
TILES = 8192
N_REP = 4


def draw_leaf_basis(key, part):
    base = jax.random.fold_in(key, 3)
    first_key, second_key, third_key, fourth_key, fifth_key = jax.random.split(base, 5)
    entries = jax.random.normal(first_key, (NLEAF, PTS, RANK), jnp.float32)
    scales = jnp.exp(jax.random.uniform(second_key, (NLEAF, RANK), jnp.float32, 0.0, math.log(3.0)))
    shared = jax.random.normal(fourth_key, (NLEAF, PTS), jnp.float32)
    loading = jax.random.uniform(fifth_key, (NLEAF, RANK), jnp.float32, 0.5, 1.5) * 0.5 * scales
    mixing = jax.random.normal(third_key, (NLEAF, RANK, RANK), jnp.float32) * (0.4 / math.sqrt(RANK))
    mixing = mixing + scales[:, :, None] * jnp.eye(RANK, dtype=jnp.float32)[None]
    independent = jnp.einsum('npr,nrs->nps', entries, mixing)
    return (independent + shared[:, :, None] * loading[:, None, :]).astype(jnp.bfloat16)


def transfer_like(key, count):
    noise = jax.random.normal(key, (count, RANK, RANK), jnp.float32)
    return noise * (0.25 / math.sqrt(RANK)) + 0.7 * jnp.eye(RANK, dtype=jnp.float32)[None]


def draw_transfer(key, part):
    return transfer_like(jax.random.fold_in(key, 5), 7 * (NLEAF // 4))


def draw_transfer_top(key, part):
    return transfer_like(jax.random.fold_in(key, 7), NLEAF // 8)


def tile_lists(key):
    base = jax.random.fold_in(key, 17)
    first_key, second_key, third_key, fourth_key = jax.random.split(base, 4)
    devices = TILES // TILE_DEV
    positions = jnp.arange(TILES, dtype=jnp.int32)
    holders = positions // TILE_DEV
    first_end = positions == TILE_DEV - 1
    last_end = positions == TILES - 1
    rows_drawn = jax.random.randint(first_key, (TILES,), 0, 7, dtype=jnp.int32)
    rows_drawn = jnp.where(first_end, 0, jnp.where(last_end, 6, rows_drawn))
    slot_pick = jax.random.randint(second_key, (TILES,), 0, 4, dtype=jnp.int32)
    slot_pick = jnp.where(first_end, 0, slot_pick)
    col_slots = jnp.where(rows_drawn < 4, slot_pick, jnp.where(rows_drawn < 6, 4 + slot_pick % 2, 6))
    offsets = jax.random.randint(third_key, (TILES,), -REACH, REACH + 1, dtype=jnp.int32)
    signs = jax.random.randint(fourth_key, (TILES,), 0, 2, dtype=jnp.int32) * 2 - 1
    offsets = jnp.where(positions % TILE_DEV == 0, signs * REACH, offsets)
    offsets = jnp.where(first_end | last_end, 0, offsets)
    target = holders + offsets
    target = jnp.where((target < 0) | (target >= devices), holders - offsets, target)
    return (rows_drawn, (7 * target + col_slots).astype(jnp.int32))


def draw_row_slot(key, part):
    return tile_lists(key)[0]


def draw_col_node(key, part):
    return tile_lists(key)[1]


def block_scale(rng, dims, cuts, smallest, top_value):
    def one(axis_at, shards_of):
        heights = jax.random.uniform(jax.random.fold_in(jax.random.fold_in(rng, 6), axis_at), (shards_of,), jnp.float32, smallest / len(cuts), top_value / len(cuts))
        return jnp.repeat(jnp.exp(heights), dims[axis_at] // shards_of).reshape((-1,) + (1,) * (len(dims) - axis_at - 1))

    factor_of = one(*cuts[0])
    for cut in cuts[1:]:
        factor_of = factor_of * one(*cut)
    return factor_of


def bell_draw(key, shape, spread, most, cuts=(), kind=jnp.bfloat16):
    drawn = spread * jax.random.normal(key, shape, jnp.float32)
    if cuts:
        drawn = drawn * block_scale(key, shape, cuts, -0.22, 0.18)
    return jnp.clip(drawn, -most, most).astype(kind)


def setup_inputs(seed: int = 0) -> dict:
    splits = jax.random.split(jax.random.key(seed), 7)
    leaf_basis = draw_leaf_basis(jax.random.fold_in(splits[6], 71), 0)
    transfer = draw_transfer(jax.random.fold_in(splits[6], 71), 0)
    transfer_top = draw_transfer_top(jax.random.fold_in(splits[6], 71), 0)
    coupling_parts = bell_draw(splits[3], (N_REP, TILES, RANK, RANK), 0.15, 1.0, ((0, 4), (1, 128)))
    row_slot = draw_row_slot(jax.random.fold_in(splits[6], 71), 0)
    col_node = draw_col_node(jax.random.fold_in(splits[6], 71), 0)
    return {"leaf_basis": leaf_basis, "transfer": transfer, "transfer_top": transfer_top, "coupling_parts": coupling_parts, "row_slot": row_slot, "col_node": col_node}


def precise(first, second):
    return jnp.dot(first.astype(jnp.float32), second.astype(jnp.float32), precision=lax.Precision.HIGHEST, preferred_element_type=jnp.float32)

def lower_solve(low_factor, rhs_mat):
    return lax.linalg.triangular_solve(low_factor, rhs_mat, left_side=True, lower=True)

def leaf_factor(leaf_rows):
    gram_sum = jnp.dot(leaf_rows.T.astype(jnp.float32), leaf_rows.astype(jnp.float32), preferred_element_type=jnp.float32) * (1.0 / PTS)
    low_factor = jnp.linalg.cholesky(gram_sum)
    identity = jnp.eye(gram_sum.shape[0], dtype=jnp.float32)
    inverse = lower_solve(low_factor, identity).T.astype(jnp.bfloat16)
    orthogonal = jnp.dot(leaf_rows.astype(jnp.float32), inverse.astype(jnp.float32), preferred_element_type=jnp.float32).astype(jnp.bfloat16)
    return (orthogonal, low_factor.T)

def combine(factor_a, factor_b, trans_a, trans_b):
    weighted_a = precise(factor_a, trans_a)
    weighted_b = precise(factor_b, trans_b)
    gram_sum = precise(weighted_a.T, weighted_a) + precise(weighted_b.T, weighted_b)
    low_factor = jnp.linalg.cholesky(gram_sum)
    new_first = lower_solve(low_factor, weighted_a.T).T
    new_second = lower_solve(low_factor, weighted_b.T).T
    return (low_factor.T, new_first, new_second)

def reference(leaf_basis, transfer, transfer_top, coupling_parts, row_slot, col_node):
    devices = transfer.shape[0] // 7
    rank_dim = transfer.shape[1]
    orthogonal, leaf_r = jax.vmap(leaf_factor)(leaf_basis)
    grouped = transfer.reshape(devices, 7, rank_dim, rank_dim)
    level_trans = [grouped[:, :4].reshape(4 * devices, rank_dim, rank_dim), grouped[:, 4:6].reshape(2 * devices, rank_dim, rank_dim), grouped[:, 6], transfer_top]
    factors = [leaf_r]
    renewed = []
    current = leaf_r
    for level_no in range(4):
        children = level_trans[level_no]
        parent, new_first, new_second = jax.vmap(combine)(current[0::2], current[1::2], children[0::2], children[1::2])
        renewed.append(jnp.stack([new_first, new_second], axis=1).reshape(children.shape))
        factors.append(parent)
        current = parent
    new_transfer = jnp.concatenate([renewed[0].reshape(devices, 4, rank_dim, rank_dim), renewed[1].reshape(devices, 2, rank_dim, rank_dim), renewed[2].reshape(devices, 1, rank_dim, rank_dim)], axis=1).reshape(7 * devices, rank_dim, rank_dim)
    factor_pool = jnp.concatenate([factors[0].reshape(devices, 4, rank_dim, rank_dim), factors[1].reshape(devices, 2, rank_dim, rank_dim), factors[2].reshape(devices, 1, rank_dim, rank_dim)], axis=1).reshape(7 * devices, rank_dim, rank_dim).astype(jnp.bfloat16)
    part_blocks = jnp.moveaxis(coupling_parts.reshape(N_REP, devices, TILE_DEV, rank_dim, rank_dim), 0, 1)
    row_blocks = row_slot.reshape(devices, TILE_DEV)
    col_blocks = col_node.reshape(devices, TILE_DEV)

    def project(block):
        holder, partials, rows_here, cols_here = block
        summed = jnp.sum(partials.astype(jnp.float32), axis=0).astype(jnp.bfloat16)
        left_factor = jnp.take(factor_pool, holder * 7 + rows_here, axis=0)
        right_factor = jnp.take(factor_pool, cols_here, axis=0)
        half_tile = jnp.einsum('kab,kbc->kac', left_factor.astype(jnp.float32), summed.astype(jnp.float32)).astype(jnp.bfloat16)
        return jnp.einsum('kab,kcb->kac', half_tile.astype(jnp.float32), right_factor.astype(jnp.float32)).astype(jnp.bfloat16)
    holders = jnp.arange(devices, dtype=jnp.int32)
    projected = lax.map(project, (holders, part_blocks, row_blocks, col_blocks))
    projected = projected.reshape(devices * TILE_DEV, rank_dim, rank_dim)
    return (orthogonal, new_transfer, renewed[3], factors[4], projected)
```

```python
import functools

import jax
import jax.numpy as jnp
from jax import lax
from jax.experimental import pallas as pl
from jax.experimental.pallas import tpu as pltpu
from jax.sharding import PartitionSpec as P

PTS = 512
N = 128
F32, BF16 = jnp.float32, jnp.bfloat16
MESH = pl.DeviceIdType.MESH
HALO = (1, -1, 2, -2)


def split3(x):
    high = x.astype(BF16)
    rest = x - high.astype(F32)
    mid = rest.astype(BF16)
    low = (rest - mid.astype(F32)).astype(BF16)
    return high, mid, low


def dot_tn(a, b):
    return lax.dot_general(a, b, (((0,), (0,)), ((), ())), preferred_element_type=F32)


def dot_nt(a, b):
    return lax.dot_general(a, b, (((1,), (1,)), ((), ())), preferred_element_type=F32)


def precise_tn(a, b):
    ah, am, al = split3(a)
    bh, bm, bl = split3(b)
    return dot_tn(
        jnp.concatenate([ah, ah, am, am, ah, al], 0),
        jnp.concatenate([bh, bm, bh, bm, bl, bh], 0),
    )


def precise_nn(a, b):
    return jnp.dot(a, b, precision=lax.Precision.HIGHEST, preferred_element_type=F32)


def precise_nt(a, b):
    return lax.dot_general(
        a, b, (((1,), (1,)), ((), ())), precision=lax.Precision.HIGHEST, preferred_element_type=F32
    )


def factor(m_ref, count, hooks=None):
    lane = lax.broadcasted_iota(jnp.int32, (1, 8, N), 2)
    sub = lax.broadcasted_iota(jnp.int32, (1, 8, N), 1)
    for j in range(N // 8):
        first = 8 * j
        rows = m_ref[:, first : first + 8, :]
        cols = [
            jnp.broadcast_to(rows[:, :, first + q : first + q + 1], (count, 8, N)) for q in range(8)
        ]
        inv = jnp.zeros((count, 8, N), F32)
        for q in range(8):
            r = 1.0 / cols[q][:, q : q + 1, :]
            inv = jnp.where(sub == q, r, inv)
            mult = jnp.where(sub > q, cols[q] * r, 0.0)
            for t in range(q + 1, 8):
                cols[t] = cols[t] - mult * cols[t][:, q : q + 1, :]
            rows = jnp.where(
                (lane == first + q) & (sub > q), -mult, rows - mult * rows[:, q : q + 1, :]
            )
        scale = jnp.sqrt(inv)
        done = rows * scale
        m_ref[:, first : first + 8, :] = done
        start = first + 8
        if start < N:
            row = first + sub
            ext = jnp.where(
                lane == row, scale, jnp.where((lane > row) & (lane < start), 0.0, done)
            )
            lanes = lax.broadcasted_iota(jnp.int32, (N - start, N), 1)
            drop = (lanes >= first) & (lanes < start)
            for m in range(count):
                update = precise_tn(done[m], ext[m])[start:]
                m_ref[m, start:, :] = jnp.where(drop, 0.0, m_ref[m, start:, :]) - update
        if hooks and j in hooks:
            hooks[j]()


def upper(x):
    r = lax.broadcasted_iota(jnp.int32, (N, N), 0)
    c = lax.broadcasted_iota(jnp.int32, (N, N), 1)
    return jnp.where(c >= r, x, 0.0)


def lower_inverse(x):
    r = lax.broadcasted_iota(jnp.int32, (N, N), 0)
    c = lax.broadcasted_iota(jnp.int32, (N, N), 1)
    return jnp.where(c < r, x, jnp.where(c == r, 1.0 / x, 0.0))


def main_kernel(
    n_leaf,
    leaf_hbm, trans_hbm, top_hbm, parts_hbm,
    orth_hbm, new_hbm, ntop_hbm, ftop_hbm, pool_hbm, sum_hbm,
    leaf_v, trans_v, top_v, mats, tops, c2, a_in, f_in, own, fwd, r_stack,
    orth_v, new_v, ntop_v, ftop_v, sum_v,
    in_sem, rs_send, rs_recv, g_send, g_recv, h_send, h_recv, out_sem,
):
    leaf, dom, rep = lax.axis_index("leaf"), lax.axis_index("dom"), lax.axis_index("rep")
    lin = (leaf * 2 + dom) * 4 + rep
    total = n_leaf * 8

    def linear(shift):
        t = lax.rem(lin + shift + total, total)
        return (lax.div(t, 8), lax.rem(lax.div(t, 4), 2), lax.rem(t, 4))

    def ring(shift):
        return lax.rem(rep + shift, 4)

    def ring_id(shift):
        return (leaf, dom, ring(shift))

    def load(src, dst, k):
        copy = pltpu.make_async_copy(src, dst, in_sem.at[k])
        copy.start()
        return copy

    load_leaf = load(leaf_hbm, leaf_v, 0)
    load_trans = load(trans_hbm, trans_v, 1)
    load_top = load(top_hbm, top_v, 2)
    load_own = load(parts_hbm.at[0, pl.ds(16 * rep, 16)], own, 3)
    load_fr = load(parts_hbm.at[0, pl.ds(16 * ring(1), 8)], fwd.at[0], 4)
    load_fl = load(parts_hbm.at[0, pl.ds(16 * ring(3) + 8, 8)], fwd.at[1], 5)

    barrier = pltpu.get_barrier_semaphore()
    for shift in (1, 2, 3):
        pl.semaphore_signal(barrier, inc=1, device_id=ring_id(shift), device_id_type=MESH)
    for shift in HALO:
        pl.semaphore_signal(barrier, inc=1, device_id=linear(shift), device_id_type=MESH)
    pl.semaphore_wait(barrier, 7)

    def remote(src, dst, send, recv, target):
        copy = pltpu.make_async_remote_copy(
            src_ref=src, dst_ref=dst, send_sem=send, recv_sem=recv,
            device_id=target, device_id_type=MESH,
        )
        copy.start()
        return copy

    def block(dest, half):
        return parts_hbm.at[0, pl.ds(16 * ring(dest) + 8 * half, 8)]

    ar = remote(block(2, 0), a_in.at[0], rs_send.at[0], rs_recv.at[0], ring_id(1))
    al = remote(block(2, 1), a_in.at[1], rs_send.at[1], rs_recv.at[1], ring_id(3))
    br = remote(block(1, 1), f_in.at[0, pl.ds(8, 8)], rs_send.at[2], rs_recv.at[2], ring_id(1))
    bl = remote(block(3, 0), f_in.at[1, pl.ds(0, 8)], rs_send.at[3], rs_recv.at[3], ring_id(3))

    load_leaf.wait()
    for i in range(4):
        u = leaf_v[i]
        mats[i] = dot_tn(u, u) * (1.0 / PTS)
    load_trans.wait()

    def lifted(g, e):
        return precise_tn(e, precise_tn(g, e))

    for p in range(2):
        mats[4 + p] = lifted(mats[2 * p], trans_v[2 * p]) + lifted(
            mats[2 * p + 1], trans_v[2 * p + 1]
        )
    mats[6] = lifted(mats[4], trans_v[4]) + lifted(mats[5], trans_v[5])
    c2[0] = lifted(mats[6], trans_v[6])
    swaps = [
        remote(c2.at[0], c2.at[s], g_send.at[s - 1], g_recv.at[s - 1], ring_id(s))
        for s in (1, 2, 3)
    ]
    second = []

    def pass_on():
        ar.wait_recv()
        load_fr.wait()
        for i in range(8):
            fwd[0, i] = (fwd[0, i].astype(F32) + a_in[0, i].astype(F32)).astype(BF16)
        second.append(
            remote(fwd.at[0], f_in.at[0, pl.ds(0, 8)], rs_send.at[4], rs_recv.at[4], ring_id(1))
        )
        al.wait_recv()
        load_fl.wait()
        for i in range(8):
            fwd[1, i] = (fwd[1, i].astype(F32) + a_in[1, i].astype(F32)).astype(BF16)
        second.append(
            remote(fwd.at[1], f_in.at[1, pl.ds(8, 8)], rs_send.at[5], rs_recv.at[5], ring_id(3))
        )

    factor(mats, 7, {10: pass_on})

    for i in range(7):
        r_stack[i] = upper(mats[i]).astype(BF16)
    halo = [
        remote(r_stack, pool_hbm.at[i], h_send.at[i], h_recv.at[i], linear(shift))
        for i, shift in enumerate(HALO)
    ]

    def store(src, dst, k):
        copy = pltpu.make_async_copy(src, dst, out_sem.at[k])
        copy.start()
        return copy

    stores = [store(r_stack, pool_hbm.at[4], 0)]

    for s in swaps:
        s.wait_recv()
    low_bit = lax.rem(rep, 2)
    high_bit = lax.div(rep, 2)
    even = low_bit == 0
    mine = c2[0] + jnp.where(even, c2[3], c2[1])
    other = c2[2] + jnp.where(even, c2[1], c2[3])
    first_node = jnp.where(high_bit == 0, mine, other)
    second_node = jnp.where(high_bit == 0, other, mine)
    load_top.wait()
    tops[0] = first_node
    tops[1] = second_node
    tops[2] = lifted(first_node, top_v[0]) + lifted(second_node, top_v[1])
    factor(tops, 3)

    for i in range(4):
        orth_v[i] = dot_nt(leaf_v[i], lower_inverse(mats[i]).astype(BF16)).astype(BF16)
    stores.append(store(orth_v, orth_hbm, 1))
    for c in range(6):
        inverse = lower_inverse(mats[4 + c // 2])
        new_v[c] = precise_nt(precise_nn(upper(mats[c]), trans_v[c]), inverse)
    own_three = jnp.where(high_bit == 0, tops[0], tops[1])
    new_v[6] = precise_nt(precise_nn(upper(mats[6]), trans_v[6]), lower_inverse(own_three))
    stores.append(store(new_v, new_hbm, 2))
    top_inverse = lower_inverse(tops[2])
    share = pl.ds(pl.multiple_of(rep * 32, 32), 32)
    row = lax.broadcasted_iota(jnp.int32, (32, N), 0) + rep * 32
    col = lax.broadcasted_iota(jnp.int32, (32, N), 1)
    keep = col >= row
    for t in range(2):
        part = jnp.where(keep, tops[t, share, :], 0.0)
        ntop_v[t] = precise_nt(precise_nn(part, top_v[t]), top_inverse)
    ftop_v[0] = jnp.where(keep, tops[2, share, :], 0.0)
    stores.append(store(ntop_v, ntop_hbm, 3))
    stores.append(store(ftop_v, ftop_hbm, 4))

    load_own.wait()
    br.wait_recv()
    bl.wait_recv()
    for s in second:
        s.wait_recv()
    for i in range(16):
        sum_v[i] = (
            own[i].astype(F32) + (f_in[0, i].astype(F32) + f_in[1, i].astype(F32))
        ).astype(BF16)
    stores.append(store(sum_v, sum_hbm, 5))
    for h in halo:
        h.wait_recv()
    for copy in [ar, al, br, bl, *swaps, *second, *halo]:
        copy.wait_send()
    for copy in stores:
        copy.wait()


def last_kernel(
    row_ref, col_ref, sum_ref, pool_ref, orth_in, new_in, ntop_in, ftop_in,
    out_ref, orth_out, new_out, ntop_out, ftop_out, sems,
):
    copies = [
        pltpu.make_async_copy(a, b, sems.at[i])
        for i, (a, b) in enumerate(
            ((orth_in, orth_out), (new_in, new_out), (ntop_in, ntop_out), (ftop_in, ftop_out))
        )
    ]
    for c in copies:
        c.start()
    me = (lax.axis_index("leaf") * 2 + lax.axis_index("dom")) * 4 + lax.axis_index("rep")
    for k in range(16):
        node = col_ref[k]
        device = lax.div(node, 7)
        slot = node - 7 * device
        shift = device - me
        place = jnp.where(shift == 0, 4, jnp.where(shift == -1, 0, jnp.where(shift == 1, 1, jnp.where(shift == -2, 2, 3))))
        left = pool_ref[4, row_ref[k]]
        right = pool_ref[place, slot]
        half = jnp.dot(left, sum_ref[k], preferred_element_type=F32).astype(BF16)
        out_ref[k] = dot_nt(half, right).astype(BF16)
    for c in copies:
        c.wait()


def per_device(n_leaf, leaf_basis, transfer, transfer_top, coupling_parts, row_slot, col_node):
    any_ = pl.BlockSpec(memory_space=pl.ANY)
    vmem = pl.BlockSpec(memory_space=pltpu.VMEM)
    smem = pl.BlockSpec(memory_space=pltpu.SMEM)
    shape = jax.ShapeDtypeStruct
    dma = pltpu.SemaphoreType.DMA
    results = [
        shape((4, PTS, N), BF16),
        shape((7, N, N), F32),
        shape((2, 32, N), F32),
        shape((1, 32, N), F32),
    ]
    *outs, pool, summed = pl.pallas_call(
        functools.partial(main_kernel, n_leaf),
        out_shape=[*results, shape((5, 7, N, N), BF16), shape((16, N, N), BF16)],
        in_specs=[any_] * 4,
        out_specs=[any_] * 6,
        scratch_shapes=[
            pltpu.VMEM((4, PTS, N), BF16),
            pltpu.VMEM((7, N, N), F32),
            pltpu.VMEM((2, N, N), F32),
            pltpu.VMEM((7, N, N), F32),
            pltpu.VMEM((3, N, N), F32),
            pltpu.VMEM((4, N, N), F32),
            pltpu.VMEM((2, 8, N, N), BF16),
            pltpu.VMEM((2, 16, N, N), BF16),
            pltpu.VMEM((16, N, N), BF16),
            pltpu.VMEM((2, 8, N, N), BF16),
            pltpu.VMEM((7, N, N), BF16),
            pltpu.VMEM((4, PTS, N), BF16),
            pltpu.VMEM((7, N, N), F32),
            pltpu.VMEM((2, 32, N), F32),
            pltpu.VMEM((1, 32, N), F32),
            pltpu.VMEM((16, N, N), BF16),
            dma((6,)), dma((6,)), dma((6,)), dma((3,)), dma((3,)), dma((4,)), dma((4,)), dma((6,)),
        ],
        compiler_params=pltpu.CompilerParams(
            collective_id=0, has_side_effects=True, vmem_limit_bytes=40 << 20
        ),
        name="factor_and_send",
    )(leaf_basis, transfer, transfer_top, coupling_parts)
    coupling, *rest = pl.pallas_call(
        last_kernel,
        out_shape=[shape((16, N, N), BF16), *results],
        in_specs=[smem, smem, vmem, vmem] + [any_] * 4,
        out_specs=[vmem] + [any_] * 4,
        scratch_shapes=[dma((4,))],
        compiler_params=pltpu.CompilerParams(vmem_limit_bytes=40 << 20),
        name="project",
    )(row_slot, col_node, summed, pool, *outs)
    return (*rest, coupling)


def solution(mesh):
    lead = P(("leaf", "dom", "rep"), None, None)
    share = P(("leaf", "dom"), "rep", None)
    return jax.shard_map(
        functools.partial(per_device, mesh.shape["leaf"]),
        mesh=mesh,
        in_specs=(
            lead,
            lead,
            P(("leaf", "dom"), None, None),
            P("rep", ("leaf", "dom"), None, None),
            P(("leaf", "dom", "rep")),
            P(("leaf", "dom", "rep")),
        ),
        out_specs=(lead, lead, share, share, lead),
        check_vma=False,
    )
```

```python
import functools

import jax
import jax.numpy as jnp
from jax import lax
from jax.experimental import pallas as pl
from jax.experimental.pallas import tpu as pltpu
from jax.sharding import PartitionSpec as P

PTS = 512
N = 128
F32, BF16 = jnp.float32, jnp.bfloat16
MESH = pl.DeviceIdType.MESH
SWAP_AT = 4
PASS_AT = 7
TOPS_AT = 9
THROUGH_AT = 3
MAIN_VMEM = 60 << 20
LAST_VMEM = 60 << 20


def split3(x):
    high = x.astype(BF16)
    rest = x - high.astype(F32)
    mid = rest.astype(BF16)
    low = (rest - mid.astype(F32)).astype(BF16)
    return high, mid, low


def dot_tn(a, b):
    return lax.dot_general(a, b, (((0,), (0,)), ((), ())), preferred_element_type=F32)


def dot_nt(a, b):
    return lax.dot_general(a, b, (((1,), (1,)), ((), ())), preferred_element_type=F32)


def precise_tn(a, b):
    ah, am, al = split3(a)
    bh, bm, bl = split3(b)
    return dot_tn(
        jnp.concatenate([ah, ah, am, am, ah, al], 0),
        jnp.concatenate([bh, bm, bh, bm, bl, bh], 0),
    )


def precise_nn(a, b):
    return jnp.dot(a, b, precision=lax.Precision.HIGHEST, preferred_element_type=F32)


def precise_nt(a, b):
    return lax.dot_general(
        a, b, (((1,), (1,)), ((), ())), precision=lax.Precision.HIGHEST, preferred_element_type=F32
    )


def eliminate(m_ref, count, j):
    lane = lax.broadcasted_iota(jnp.int32, (1, 8, N), 2)
    sub = lax.broadcasted_iota(jnp.int32, (1, 8, N), 1)
    first = 8 * j
    rows = m_ref[:, first : first + 8, :]
    cols = [
        jnp.broadcast_to(rows[:, :, first + q : first + q + 1], (count, 8, N)) for q in range(8)
    ]
    inv = jnp.zeros((count, 8, N), F32)
    for q in range(8):
        r = 1.0 / cols[q][:, q : q + 1, :]
        inv = jnp.where(sub == q, r, inv)
        mult = jnp.where(sub > q, cols[q] * r, 0.0)
        for t in range(q + 1, 8):
            cols[t] = cols[t] - mult * cols[t][:, q : q + 1, :]
        rows = jnp.where(
            (lane == first + q) & (sub > q), -mult, rows - mult * rows[:, q : q + 1, :]
        )
    scale = jnp.sqrt(inv)
    done = rows * scale
    m_ref[:, first : first + 8, :] = done
    start = first + 8
    if start < N:
        row = first + sub
        ext = jnp.where(lane == row, scale, jnp.where((lane > row) & (lane < start), 0.0, done))
        lanes = lax.broadcasted_iota(jnp.int32, (N - start, N), 1)
        drop = (lanes >= first) & (lanes < start)
        for m in range(count):
            update = precise_tn(done[m], ext[m])[start:]
            m_ref[m, start:, :] = jnp.where(drop, 0.0, m_ref[m, start:, :]) - update


def upper(x):
    r = lax.broadcasted_iota(jnp.int32, (N, N), 0)
    c = lax.broadcasted_iota(jnp.int32, (N, N), 1)
    return jnp.where(c >= r, x, 0.0)


def lower_inverse(x):
    r = lax.broadcasted_iota(jnp.int32, (N, N), 0)
    c = lax.broadcasted_iota(jnp.int32, (N, N), 1)
    return jnp.where(c < r, x, jnp.where(c == r, 1.0 / x, 0.0))


def pack(ups):
    strips, halves = [], []
    for u in ups:
        strips.append(u[0:16])
        for i in (1, 2, 3):
            low = u[128 - 16 * i : 144 - 16 * i]
            strips.append(u[16 * i : 16 * i + 16] + pltpu.roll(low, 16 * i, 1))
        halves.append(u[64:80])
    for m in range(0, len(halves) - 1, 2):
        strips.append(halves[m] + pltpu.roll(halves[m + 1], 64, 1))
    if len(halves) % 2:
        strips.append(halves[-1])
    return strips


def main_kernel(
    n_leaf,
    row_ref, leaf_hbm, trans_hbm, top_hbm, parts_hbm,
    orth_hbm, new_hbm, ntop_hbm, ftop_hbm, pool_hbm, half_hbm,
    leaf_v, trans_v, top_v, mats, tops, c2, a_in, f_in, own, fwd, r_stack, packed,
    orth_v, new_v, ntop_v, ftop_v, half_v,
    in_sem, rs_send, rs_recv, g_send, g_recv, h_send, h_recv, out_sem,
):
    leaf, dom, rep = lax.axis_index("leaf"), lax.axis_index("dom"), lax.axis_index("rep")
    lin = (leaf * 2 + dom) * 4 + rep
    total = n_leaf * 8

    def linear(shift):
        t = lax.rem(lin + shift + total, total)
        return (lax.div(t, 8), lax.rem(lax.div(t, 4), 2), lax.rem(t, 4))

    def ring(shift):
        return lax.rem(rep + shift, 4)

    def ring_id(shift):
        return (leaf, dom, ring(shift))

    def load(src, dst, k):
        copy = pltpu.make_async_copy(src, dst, in_sem.at[k])
        copy.start()
        return copy

    barrier = pltpu.get_barrier_semaphore()
    for target in (ring_id(1), ring_id(3), linear(1), linear(-1)):
        pl.semaphore_signal(barrier, inc=1, device_id=target, device_id_type=MESH)

    load_leaf = load(leaf_hbm, leaf_v, 0)
    load_trans = load(trans_hbm, trans_v, 1)
    load_top = load(top_hbm, top_v, 2)
    load_own = load(parts_hbm.at[0, pl.ds(16 * rep, 16)], own, 3)
    load_fr = load(parts_hbm.at[0, pl.ds(16 * ring(1), 8)], fwd.at[0], 4)
    load_fl = load(parts_hbm.at[0, pl.ds(16 * ring(3) + 8, 8)], fwd.at[1], 5)
    pl.semaphore_wait(barrier, 4)

    def remote(src, dst, send, recv, target):
        copy = pltpu.make_async_remote_copy(
            src_ref=src, dst_ref=dst, send_sem=send, recv_sem=recv,
            device_id=target, device_id_type=MESH,
        )
        copy.start()
        return copy

    def block(dest, half):
        return parts_hbm.at[0, pl.ds(16 * ring(dest) + 8 * half, 8)]

    ar = remote(block(2, 0), a_in.at[0], rs_send.at[0], rs_recv.at[0], ring_id(1))
    al = remote(block(2, 1), a_in.at[1], rs_send.at[1], rs_recv.at[1], ring_id(3))

    load_leaf.wait()
    for i in range(4):
        u = leaf_v[i]
        mats[i] = dot_tn(u, u) * (1.0 / PTS)
    load_trans.wait()

    def lifted(g, e):
        return precise_tn(e, precise_tn(g, e))

    for p in range(2):
        mats[4 + p] = lifted(mats[2 * p], trans_v[2 * p]) + lifted(
            mats[2 * p + 1], trans_v[2 * p + 1]
        )
    mats[6] = lifted(mats[4], trans_v[4]) + lifted(mats[5], trans_v[5])
    c2[0] = lifted(mats[6], trans_v[6])
    low_bit = lax.rem(rep, 2)
    swaps = [
        remote(c2.at[0], c2.at[1], g_send.at[0], g_recv.at[0], (leaf, dom, rep + 1 - 2 * low_bit))
    ]
    br = remote(block(1, 1), f_in.at[0, pl.ds(8, 8)], rs_send.at[2], rs_recv.at[2], ring_id(1))
    bl = remote(block(3, 0), f_in.at[1, pl.ds(0, 8)], rs_send.at[3], rs_recv.at[3], ring_id(3))
    second = []

    def swap_pairs():
        swaps[0].wait_recv()
        c2[2] = c2[0] + c2[1]
        swaps.append(
            remote(c2.at[2], c2.at[3], g_send.at[1], g_recv.at[1], (leaf, dom, 3 - rep))
        )

    def pass_on():
        ar.wait_recv()
        load_fr.wait()
        for i in range(8):
            fwd[0, i] = (fwd[0, i].astype(F32) + a_in[0, i].astype(F32)).astype(BF16)
        second.append(
            remote(fwd.at[0], f_in.at[0, pl.ds(0, 8)], rs_send.at[4], rs_recv.at[4], ring_id(1))
        )
        al.wait_recv()
        load_fl.wait()
        for i in range(8):
            fwd[1, i] = (fwd[1, i].astype(F32) + a_in[1, i].astype(F32)).astype(BF16)
        second.append(
            remote(fwd.at[1], f_in.at[1, pl.ds(8, 8)], rs_send.at[5], rs_recv.at[5], ring_id(3))
        )

    first_half = rep < 2

    def top_grams():
        swaps[1].wait_recv()
        load_top.wait()
        first_node = jnp.where(first_half, c2[2], c2[3])
        second_node = jnp.where(first_half, c2[3], c2[2])
        tops[0] = first_node
        tops[1] = second_node
        tops[2] = lifted(first_node, top_v[0]) + lifted(second_node, top_v[1])

    for j in range(N // 8):
        if j == SWAP_AT:
            swap_pairs()
        if j == PASS_AT:
            pass_on()
        if j == TOPS_AT:
            top_grams()
        eliminate(mats, 7, j)
        if j >= TOPS_AT:
            eliminate(tops, 3, j - TOPS_AT)

    ups = [upper(mats[i]) for i in range(7)]
    for i, strip in enumerate(pack(ups)):
        packed[i] = strip.astype(BF16)
    halo = [
        remote(packed, pool_hbm.at[i], h_send.at[i], h_recv.at[i], linear(shift))
        for i, shift in enumerate((1, -1))
    ]
    for i in range(7):
        r_stack[i] = ups[i].astype(BF16)

    def store(src, dst, k):
        copy = pltpu.make_async_copy(src, dst, out_sem.at[k])
        copy.start()
        return copy

    stores = [store(packed, pool_hbm.at[4], 0)]

    def forward():
        for i, shift in enumerate((1, -1)):
            halo[i].wait_recv()
            halo.append(
                remote(pool_hbm.at[i], pool_hbm.at[2 + i], h_send.at[2 + i], h_recv.at[2 + i], linear(shift))
            )

    def sums():
        load_own.wait()
        for s in [br, bl, *second]:
            s.wait_recv()
        for i in range(16):
            total_i = own[i].astype(F32) + (f_in[0, i].astype(F32) + f_in[1, i].astype(F32))
            half_v[i] = jnp.dot(
                r_stack[row_ref[i]], total_i.astype(BF16), preferred_element_type=F32
            ).astype(BF16)
        stores.append(store(half_v, half_hbm, 5))

    for j in range(N // 8 - TOPS_AT, N // 8):
        eliminate(tops, 3, j)

    for i in range(4):
        orth_v[i] = dot_nt(leaf_v[i], lower_inverse(mats[i]).astype(BF16)).astype(BF16)
    stores.append(store(orth_v, orth_hbm, 1))
    for c in range(6):
        inverse = lower_inverse(mats[4 + c // 2])
        new_v[c] = precise_nt(precise_nn(upper(mats[c]), trans_v[c]), inverse)
    own_three = jnp.where(first_half, tops[0], tops[1])
    new_v[6] = precise_nt(precise_nn(upper(mats[6]), trans_v[6]), lower_inverse(own_three))
    stores.append(store(new_v, new_hbm, 2))
    top_inverse = lower_inverse(tops[2])
    share = pl.ds(pl.multiple_of(rep * 32, 32), 32)
    row = lax.broadcasted_iota(jnp.int32, (32, N), 0) + rep * 32
    col = lax.broadcasted_iota(jnp.int32, (32, N), 1)
    keep = col >= row
    for t in range(2):
        part = jnp.where(keep, tops[t, share, :], 0.0)
        ntop_v[t] = precise_nt(precise_nn(part, top_v[t]), top_inverse)
    ftop_v[0] = jnp.where(keep, tops[2, share, :], 0.0)
    stores.append(store(ntop_v, ntop_hbm, 3))
    stores.append(store(ftop_v, ftop_hbm, 4))

    forward()
    sums()
    for h in halo[2:]:
        h.wait_recv()
    for copy in [ar, al, br, bl, *swaps, *second, *halo]:
        copy.wait_send()
    for copy in stores:
        copy.wait()


def last_kernel(
    col_ref, half_hbm, pool_hbm, orth_in, new_in, ntop_in, ftop_in,
    out_hbm, orth_out, new_out, ntop_out, ftop_out,
    half_ref, pool_ref, orth_v, new_v, ntop_v, ftop_v, out_v, in_sems, sems,
):
    loads = [
        pltpu.make_async_copy(a, b, in_sems.at[i])
        for i, (a, b) in enumerate(
            (
                (half_hbm, half_ref), (pool_hbm, pool_ref),
                (orth_in, orth_v), (new_in, new_v), (ntop_in, ntop_v), (ftop_in, ftop_v),
            )
        )
    ]
    for c in loads:
        c.start()
    for c in loads[:2]:
        c.wait()
    copies = []

    def through():
        for i, (a, b) in enumerate(
            ((orth_v, orth_out), (new_v, new_out), (ntop_v, ntop_out), (ftop_v, ftop_out))
        ):
            loads[2 + i].wait()
            c = pltpu.make_async_copy(a, b, sems.at[i])
            c.start()
            copies.append(c)

    me = (lax.axis_index("leaf") * 2 + lax.axis_index("dom")) * 4 + lax.axis_index("rep")
    lane = lax.broadcasted_iota(jnp.int32, (16, N), 1)

    def keep(x, first):
        return jnp.where(lane >= first, x, 0.0)

    for k in range(16):
        node = col_ref[k]
        device = lax.div(node, 7)
        slot = node - 7 * device
        shift = device - me
        place = jnp.where(
            shift == 0, 4, jnp.where(shift > 0, 2 * shift - 1, -2 * shift - 2)
        )
        strip = [pool_ref[place, 4 * slot + i].astype(F32) for i in range(4)]
        pair = pool_ref[place, 28 + lax.div(slot, 2)].astype(F32)
        pair = jnp.where(lax.rem(slot, 2) == 1, pltpu.roll(pair, 64, 1), pair)
        right = jnp.concatenate(
            [strip[0]]
            + [keep(strip[i], 16 * i) for i in (1, 2, 3)]
            + [keep(pair, 64)]
            + [keep(pltpu.roll(strip[i], N - 16 * i, 1), N - 16 * i) for i in (3, 2, 1)],
            0,
        ).astype(BF16)
        out_v[k] = dot_nt(half_ref[k], right).astype(BF16)
        if k % 4 == 3:
            part = pl.ds(k - 3, 4)
            c = pltpu.make_async_copy(out_v.at[part], out_hbm.at[part], sems.at[4 + k // 4])
            c.start()
            copies.append(c)
        if k == THROUGH_AT:
            through()
    for c in copies:
        c.wait()


def per_device(n_leaf, leaf_basis, transfer, transfer_top, coupling_parts, row_slot, col_node):
    any_ = pl.BlockSpec(memory_space=pl.ANY)
    smem = pl.BlockSpec(memory_space=pltpu.SMEM)
    shape = jax.ShapeDtypeStruct
    dma = pltpu.SemaphoreType.DMA
    results = [
        shape((4, PTS, N), BF16),
        shape((7, N, N), F32),
        shape((2, 32, N), F32),
        shape((1, 32, N), F32),
    ]
    *outs, pool, half = pl.pallas_call(
        functools.partial(main_kernel, n_leaf),
        out_shape=[*results, shape((5, 32, 16, N), BF16), shape((16, N, N), BF16)],
        in_specs=[smem] + [any_] * 4,
        out_specs=[any_] * 6,
        scratch_shapes=[
            pltpu.VMEM((4, PTS, N), BF16),
            pltpu.VMEM((7, N, N), F32),
            pltpu.VMEM((2, N, N), F32),
            pltpu.VMEM((7, N, N), F32),
            pltpu.VMEM((3, N, N), F32),
            pltpu.VMEM((4, N, N), F32),
            pltpu.VMEM((2, 8, N, N), BF16),
            pltpu.VMEM((2, 16, N, N), BF16),
            pltpu.VMEM((16, N, N), BF16),
            pltpu.VMEM((2, 8, N, N), BF16),
            pltpu.VMEM((7, N, N), BF16),
            pltpu.VMEM((32, 16, N), BF16),
            pltpu.VMEM((4, PTS, N), BF16),
            pltpu.VMEM((7, N, N), F32),
            pltpu.VMEM((2, 32, N), F32),
            pltpu.VMEM((1, 32, N), F32),
            pltpu.VMEM((16, N, N), BF16),
            dma((6,)), dma((6,)), dma((6,)), dma((2,)), dma((2,)), dma((4,)), dma((4,)), dma((6,)),
        ],
        compiler_params=pltpu.CompilerParams(
            collective_id=0, has_side_effects=True, vmem_limit_bytes=MAIN_VMEM
        ),
        name="factor_and_send",
    )(row_slot, leaf_basis, transfer, transfer_top, coupling_parts)
    coupling, *rest = pl.pallas_call(
        last_kernel,
        out_shape=[shape((16, N, N), BF16), *results],
        in_specs=[smem] + [any_] * 6,
        out_specs=[any_] * 5,
        scratch_shapes=[
            pltpu.VMEM((16, N, N), BF16),
            pltpu.VMEM((5, 32, 16, N), BF16),
            pltpu.VMEM((4, PTS, N), BF16),
            pltpu.VMEM((7, N, N), F32),
            pltpu.VMEM((2, 32, N), F32),
            pltpu.VMEM((1, 32, N), F32),
            pltpu.VMEM((16, N, N), BF16),
            dma((6,)),
            dma((8,)),
        ],
        compiler_params=pltpu.CompilerParams(vmem_limit_bytes=LAST_VMEM),
        name="project",
    )(col_node, half, pool, *outs)
    return (*rest, coupling)


def solution(mesh):
    lead = P(("leaf", "dom", "rep"), None, None)
    share = P(("leaf", "dom"), "rep", None)
    return jax.shard_map(
        functools.partial(per_device, mesh.shape["leaf"]),
        mesh=mesh,
        in_specs=(
            lead,
            lead,
            P(("leaf", "dom"), None, None),
            P("rep", ("leaf", "dom"), None, None),
            P(("leaf", "dom", "rep")),
            P(("leaf", "dom", "rep")),
        ),
        out_specs=(lead, lead, share, share, lead),
        check_vma=False,
    )
```

```python
import functools

import jax
import jax.numpy as jnp
from jax import lax
from jax.experimental import pallas as pl
from jax.experimental.pallas import tpu as pltpu
from jax.sharding import PartitionSpec as P

PTS = 512
N = 128
F32, BF16 = jnp.float32, jnp.bfloat16
MESH = pl.DeviceIdType.MESH
SWAP_AT = 4
PASS_AT = 8
DIRECT_AT = 16
TOPS_AT = 9
THROUGH_AT = 3
FORWARD_AT = 16
EARLY = 1
MAIN_VMEM = 60 << 20
LAST_VMEM = 60 << 20


def split3(x):
    high = x.astype(BF16)
    rest = x - high.astype(F32)
    mid = rest.astype(BF16)
    low = (rest - mid.astype(F32)).astype(BF16)
    return high, mid, low


def dot_tn(a, b):
    return lax.dot_general(a, b, (((0,), (0,)), ((), ())), preferred_element_type=F32)


def dot_nt(a, b):
    return lax.dot_general(a, b, (((1,), (1,)), ((), ())), preferred_element_type=F32)


def precise_tn(a, b):
    ah, am, al = split3(a)
    bh, bm, bl = split3(b)
    return dot_tn(
        jnp.concatenate([ah, ah, am, am, ah, al], 0),
        jnp.concatenate([bh, bm, bh, bm, bl, bh], 0),
    )


def precise_nn(a, b):
    return jnp.dot(a, b, precision=lax.Precision.HIGHEST, preferred_element_type=F32)


def precise_nt(a, b):
    return lax.dot_general(
        a, b, (((1,), (1,)), ((), ())), precision=lax.Precision.HIGHEST, preferred_element_type=F32
    )


def eliminate(m_ref, count, j):
    lane = lax.broadcasted_iota(jnp.int32, (1, 8, N), 2)
    sub = lax.broadcasted_iota(jnp.int32, (1, 8, N), 1)
    first = 8 * j
    rows = m_ref[:, first : first + 8, :]
    cols = [
        jnp.broadcast_to(rows[:, :, first + q : first + q + 1], (count, 8, N)) for q in range(8)
    ]
    inv = jnp.zeros((count, 8, N), F32)
    for q in range(8):
        r = 1.0 / cols[q][:, q : q + 1, :]
        inv = jnp.where(sub == q, r, inv)
        mult = jnp.where(sub > q, cols[q] * r, 0.0)
        for t in range(q + 1, 8):
            cols[t] = cols[t] - mult * cols[t][:, q : q + 1, :]
        rows = jnp.where(
            (lane == first + q) & (sub > q), -mult, rows - mult * rows[:, q : q + 1, :]
        )
    scale = jnp.sqrt(inv)
    done = rows * scale
    m_ref[:, first : first + 8, :] = done
    start = first + 8
    if start < N:
        row = first + sub
        ext = jnp.where(lane == row, scale, jnp.where((lane > row) & (lane < start), 0.0, done))
        lanes = lax.broadcasted_iota(jnp.int32, (N - start, N), 1)
        drop = (lanes >= first) & (lanes < start)
        for m in range(count):
            update = precise_tn(done[m], ext[m])[start:]
            m_ref[m, start:, :] = jnp.where(drop, 0.0, m_ref[m, start:, :]) - update


def upper(x):
    r = lax.broadcasted_iota(jnp.int32, (N, N), 0)
    c = lax.broadcasted_iota(jnp.int32, (N, N), 1)
    return jnp.where(c >= r, x, 0.0)


def lower_inverse(x):
    r = lax.broadcasted_iota(jnp.int32, (N, N), 0)
    c = lax.broadcasted_iota(jnp.int32, (N, N), 1)
    return jnp.where(c < r, x, jnp.where(c == r, 1.0 / x, 0.0))


def pack(ups):
    strips, halves = [], []
    for u in ups:
        strips.append(u[0:16])
        for i in (1, 2, 3):
            low = u[128 - 16 * i : 144 - 16 * i]
            strips.append(u[16 * i : 16 * i + 16] + pltpu.roll(low, 16 * i, 1))
        halves.append(u[64:80])
    for m in range(0, len(halves) - 1, 2):
        strips.append(halves[m] + pltpu.roll(halves[m + 1], 64, 1))
    if len(halves) % 2:
        strips.append(halves[-1])
    return strips


def main_kernel(
    n_leaf,
    row_ref, leaf_hbm, trans_hbm, top_hbm, parts_hbm,
    orth_hbm, new_hbm, ntop_hbm, ftop_hbm, pool_hbm, half_hbm,
    leaf_v, trans_v, top_v, mats, tops, c2, a_in, f_in, own, fwd, r_stack, packed,
    orth_v, new_v, ntop_v, ftop_v, half_v,
    in_sem, rs_send, rs_recv, g_send, g_recv, h_send, h_recv, out_sem, hello,
):
    leaf, dom, rep = lax.axis_index("leaf"), lax.axis_index("dom"), lax.axis_index("rep")
    lin = (leaf * 2 + dom) * 4 + rep
    total = n_leaf * 8

    def linear(shift):
        t = lax.rem(lin + shift + total, total)
        return (lax.div(t, 8), lax.rem(lax.div(t, 4), 2), lax.rem(t, 4))

    def ring(shift):
        return lax.rem(rep + shift, 4)

    def ring_id(shift):
        return (leaf, dom, ring(shift))

    def load(src, dst, k):
        copy = pltpu.make_async_copy(src, dst, in_sem.at[k])
        copy.start()
        return copy

    barrier = pltpu.get_barrier_semaphore()
    for target in (ring_id(1), ring_id(3)):
        pl.semaphore_signal(barrier, inc=1, device_id=target, device_id_type=MESH)

    @pl.when(rep == 0)
    def _():
        pl.semaphore_signal(barrier, inc=1, device_id=linear(-1), device_id_type=MESH)

    load_leaf = load(leaf_hbm, leaf_v, 0)
    load_trans = load(trans_hbm, trans_v, 1)
    load_top = load(top_hbm, top_v, 2)
    load_own = load(parts_hbm.at[0, pl.ds(16 * rep, 16)], own, 3)
    load_fr = load(parts_hbm.at[0, pl.ds(16 * ring(1), 8)], fwd.at[0], 4)
    load_fl = load(parts_hbm.at[0, pl.ds(16 * ring(3) + 8, 8)], fwd.at[1], 5)

    def lifted(g, e):
        return precise_tn(e, precise_tn(g, e))

    def leaf_grams():
        load_leaf.wait()
        for i in range(4):
            u = leaf_v[i]
            mats[i] = dot_tn(u, u) * (1.0 / PTS)
        load_trans.wait()

    def first_level():
        for p in range(2):
            mats[4 + p] = lifted(mats[2 * p], trans_v[2 * p]) + lifted(
                mats[2 * p + 1], trans_v[2 * p + 1]
            )

    def second_level():
        mats[6] = lifted(mats[4], trans_v[4]) + lifted(mats[5], trans_v[5])
        c2[0] = lifted(mats[6], trans_v[6])

    grams = [leaf_grams, first_level, second_level]
    for g in grams[:EARLY]:
        g()
    pl.semaphore_wait(barrier, 2 + lax.div(rep, 3))

    @pl.when(rep == 3)
    def _():
        pl.semaphore_signal(hello, inc=1, device_id=linear(1), device_id_type=MESH)

    def remote(src, dst, send, recv, target):
        copy = pltpu.make_async_remote_copy(
            src_ref=src, dst_ref=dst, send_sem=send, recv_sem=recv,
            device_id=target, device_id_type=MESH,
        )
        copy.start()
        return copy

    def block(dest, half):
        return parts_hbm.at[0, pl.ds(16 * ring(dest) + 8 * half, 8)]

    ar = remote(block(2, 0), a_in.at[0], rs_send.at[0], rs_recv.at[0], ring_id(1))
    al = remote(block(2, 1), a_in.at[1], rs_send.at[1], rs_recv.at[1], ring_id(3))

    for g in grams[EARLY:]:
        g()
    low_bit = lax.rem(rep, 2)
    swaps = [
        remote(c2.at[0], c2.at[1], g_send.at[0], g_recv.at[0], (leaf, dom, rep + 1 - 2 * low_bit))
    ]
    direct = []

    def send_direct():
        direct.append(
            remote(block(1, 1), f_in.at[0, pl.ds(8, 8)], rs_send.at[2], rs_recv.at[2], ring_id(1))
        )
        direct.append(
            remote(block(3, 0), f_in.at[1, pl.ds(0, 8)], rs_send.at[3], rs_recv.at[3], ring_id(3))
        )

    if DIRECT_AT == -1:
        send_direct()
    second = []

    def swap_pairs():
        swaps[0].wait_recv()
        c2[2] = c2[0] + c2[1]
        swaps.append(
            remote(c2.at[2], c2.at[3], g_send.at[1], g_recv.at[1], (leaf, dom, 3 - rep))
        )

    def pass_on():
        ar.wait_recv()
        load_fr.wait()
        for i in range(8):
            fwd[0, i] = (fwd[0, i].astype(F32) + a_in[0, i].astype(F32)).astype(BF16)
        second.append(
            remote(fwd.at[0], f_in.at[0, pl.ds(0, 8)], rs_send.at[4], rs_recv.at[4], ring_id(1))
        )
        al.wait_recv()
        load_fl.wait()
        for i in range(8):
            fwd[1, i] = (fwd[1, i].astype(F32) + a_in[1, i].astype(F32)).astype(BF16)
        second.append(
            remote(fwd.at[1], f_in.at[1, pl.ds(8, 8)], rs_send.at[5], rs_recv.at[5], ring_id(3))
        )

    first_half = rep < 2

    def top_grams():
        swaps[1].wait_recv()
        load_top.wait()
        first_node = jnp.where(first_half, c2[2], c2[3])
        second_node = jnp.where(first_half, c2[3], c2[2])
        tops[0] = first_node
        tops[1] = second_node
        tops[2] = lifted(first_node, top_v[0]) + lifted(second_node, top_v[1])

    for j in range(N // 8):
        if j == SWAP_AT:
            swap_pairs()
        if j == PASS_AT:
            pass_on()
        if j == TOPS_AT:
            top_grams()
        if j == DIRECT_AT:
            send_direct()
        eliminate(mats, 7, j)
        if j >= TOPS_AT:
            eliminate(tops, 3, j - TOPS_AT)

    ups = [upper(mats[i]) for i in range(7)]
    for i, strip in enumerate(pack(ups)):
        packed[i] = strip.astype(BF16)

    @pl.when(rep == 0)
    def _():
        pl.semaphore_wait(hello, 1)

    halo = [
        remote(packed, pool_hbm.at[i], h_send.at[i], h_recv.at[i], linear(shift))
        for i, shift in enumerate((1, -1))
    ]
    if DIRECT_AT == 16:
        send_direct()
    for i in range(7):
        r_stack[i] = ups[i].astype(BF16)

    def store(src, dst, k):
        copy = pltpu.make_async_copy(src, dst, out_sem.at[k])
        copy.start()
        return copy

    stores = [store(packed, pool_hbm.at[4], 0)]

    def forward():
        for i, shift in enumerate((1, -1)):
            halo[i].wait_recv()
            halo.append(
                remote(pool_hbm.at[i], pool_hbm.at[2 + i], h_send.at[2 + i], h_recv.at[2 + i], linear(shift))
            )

    def sums():
        load_own.wait()
        for s in [*direct, *second]:
            s.wait_recv()
        for i in range(16):
            total_i = own[i].astype(F32) + (f_in[0, i].astype(F32) + f_in[1, i].astype(F32))
            half_v[i] = jnp.dot(
                r_stack[row_ref[i]], total_i.astype(BF16), preferred_element_type=F32
            ).astype(BF16)
        stores.append(store(half_v, half_hbm, 5))

    for j in range(N // 8 - TOPS_AT, N // 8):
        if j == FORWARD_AT:
            forward()
        eliminate(tops, 3, j)
    if FORWARD_AT == 16:
        forward()

    for i in range(4):
        orth_v[i] = dot_nt(leaf_v[i], lower_inverse(mats[i]).astype(BF16)).astype(BF16)
    stores.append(store(orth_v, orth_hbm, 1))
    for c in range(6):
        inverse = lower_inverse(mats[4 + c // 2])
        new_v[c] = precise_nt(precise_nn(upper(mats[c]), trans_v[c]), inverse)
    own_three = jnp.where(first_half, tops[0], tops[1])
    new_v[6] = precise_nt(precise_nn(upper(mats[6]), trans_v[6]), lower_inverse(own_three))
    stores.append(store(new_v, new_hbm, 2))
    top_inverse = lower_inverse(tops[2])
    share = pl.ds(pl.multiple_of(rep * 32, 32), 32)
    row = lax.broadcasted_iota(jnp.int32, (32, N), 0) + rep * 32
    col = lax.broadcasted_iota(jnp.int32, (32, N), 1)
    keep = col >= row
    for t in range(2):
        part = jnp.where(keep, tops[t, share, :], 0.0)
        ntop_v[t] = precise_nt(precise_nn(part, top_v[t]), top_inverse)
    ftop_v[0] = jnp.where(keep, tops[2, share, :], 0.0)
    stores.append(store(ntop_v, ntop_hbm, 3))
    stores.append(store(ftop_v, ftop_hbm, 4))

    if FORWARD_AT == 17:
        forward()
    sums()
    for h in halo[2:]:
        h.wait_recv()
    for copy in [ar, al, *direct, *swaps, *second, *halo]:
        copy.wait_send()
    for copy in stores:
        copy.wait()


def last_kernel(
    col_ref, half_hbm, pool_hbm, orth_in, new_in, ntop_in, ftop_in,
    out_hbm, orth_out, new_out, ntop_out, ftop_out,
    half_ref, pool_ref, orth_v, new_v, ntop_v, ftop_v, out_v, in_sems, sems,
):
    loads = [
        pltpu.make_async_copy(a, b, in_sems.at[i])
        for i, (a, b) in enumerate(
            (
                (half_hbm, half_ref), (pool_hbm, pool_ref),
                (orth_in, orth_v), (new_in, new_v), (ntop_in, ntop_v), (ftop_in, ftop_v),
            )
        )
    ]
    for c in loads:
        c.start()
    for c in loads[:2]:
        c.wait()
    copies = []

    def through():
        for i, (a, b) in enumerate(
            ((orth_v, orth_out), (new_v, new_out), (ntop_v, ntop_out), (ftop_v, ftop_out))
        ):
            loads[2 + i].wait()
            c = pltpu.make_async_copy(a, b, sems.at[i])
            c.start()
            copies.append(c)

    me = (lax.axis_index("leaf") * 2 + lax.axis_index("dom")) * 4 + lax.axis_index("rep")
    lane = lax.broadcasted_iota(jnp.int32, (16, N), 1)

    def keep(x, first):
        return jnp.where(lane >= first, x, 0.0)

    for k in range(16):
        node = col_ref[k]
        device = lax.div(node, 7)
        slot = node - 7 * device
        shift = device - me
        place = jnp.where(
            shift == 0, 4, jnp.where(shift > 0, 2 * shift - 1, -2 * shift - 2)
        )
        strip = [pool_ref[place, 4 * slot + i].astype(F32) for i in range(4)]
        pair = pool_ref[place, 28 + lax.div(slot, 2)].astype(F32)
        pair = jnp.where(lax.rem(slot, 2) == 1, pltpu.roll(pair, 64, 1), pair)
        right = jnp.concatenate(
            [strip[0]]
            + [keep(strip[i], 16 * i) for i in (1, 2, 3)]
            + [keep(pair, 64)]
            + [keep(pltpu.roll(strip[i], N - 16 * i, 1), N - 16 * i) for i in (3, 2, 1)],
            0,
        ).astype(BF16)
        out_v[k] = dot_nt(half_ref[k], right).astype(BF16)
        if k % 4 == 3:
            part = pl.ds(k - 3, 4)
            c = pltpu.make_async_copy(out_v.at[part], out_hbm.at[part], sems.at[4 + k // 4])
            c.start()
            copies.append(c)
        if k == THROUGH_AT:
            through()
    for c in copies:
        c.wait()


def per_device(n_leaf, leaf_basis, transfer, transfer_top, coupling_parts, row_slot, col_node):
    any_ = pl.BlockSpec(memory_space=pl.ANY)
    smem = pl.BlockSpec(memory_space=pltpu.SMEM)
    shape = jax.ShapeDtypeStruct
    dma = pltpu.SemaphoreType.DMA
    results = [
        shape((4, PTS, N), BF16),
        shape((7, N, N), F32),
        shape((2, 32, N), F32),
        shape((1, 32, N), F32),
    ]
    *outs, pool, half = pl.pallas_call(
        functools.partial(main_kernel, n_leaf),
        out_shape=[*results, shape((5, 32, 16, N), BF16), shape((16, N, N), BF16)],
        in_specs=[smem] + [any_] * 4,
        out_specs=[any_] * 6,
        scratch_shapes=[
            pltpu.VMEM((4, PTS, N), BF16),
            pltpu.VMEM((7, N, N), F32),
            pltpu.VMEM((2, N, N), F32),
            pltpu.VMEM((7, N, N), F32),
            pltpu.VMEM((3, N, N), F32),
            pltpu.VMEM((4, N, N), F32),
            pltpu.VMEM((2, 8, N, N), BF16),
            pltpu.VMEM((2, 16, N, N), BF16),
            pltpu.VMEM((16, N, N), BF16),
            pltpu.VMEM((2, 8, N, N), BF16),
            pltpu.VMEM((7, N, N), BF16),
            pltpu.VMEM((32, 16, N), BF16),
            pltpu.VMEM((4, PTS, N), BF16),
            pltpu.VMEM((7, N, N), F32),
            pltpu.VMEM((2, 32, N), F32),
            pltpu.VMEM((1, 32, N), F32),
            pltpu.VMEM((16, N, N), BF16),
            dma((6,)), dma((6,)), dma((6,)), dma((2,)), dma((2,)), dma((4,)), dma((4,)), dma((6,)),
            pltpu.SemaphoreType.REGULAR,
        ],
        compiler_params=pltpu.CompilerParams(
            collective_id=0, has_side_effects=True, vmem_limit_bytes=MAIN_VMEM
        ),
        name="factor_and_send",
    )(row_slot, leaf_basis, transfer, transfer_top, coupling_parts)
    coupling, *rest = pl.pallas_call(
        last_kernel,
        out_shape=[shape((16, N, N), BF16), *results],
        in_specs=[smem] + [any_] * 6,
        out_specs=[any_] * 5,
        scratch_shapes=[
            pltpu.VMEM((16, N, N), BF16),
            pltpu.VMEM((5, 32, 16, N), BF16),
            pltpu.VMEM((4, PTS, N), BF16),
            pltpu.VMEM((7, N, N), F32),
            pltpu.VMEM((2, 32, N), F32),
            pltpu.VMEM((1, 32, N), F32),
            pltpu.VMEM((16, N, N), BF16),
            dma((6,)),
            dma((8,)),
        ],
        compiler_params=pltpu.CompilerParams(vmem_limit_bytes=LAST_VMEM),
        name="project",
    )(col_node, half, pool, *outs)
    return (*rest, coupling)


def solution(mesh):
    lead = P(("leaf", "dom", "rep"), None, None)
    share = P(("leaf", "dom"), "rep", None)
    return jax.shard_map(
        functools.partial(per_device, mesh.shape["leaf"]),
        mesh=mesh,
        in_specs=(
            lead,
            lead,
            P(("leaf", "dom"), None, None),
            P("rep", ("leaf", "dom"), None, None),
            P(("leaf", "dom", "rep")),
            P(("leaf", "dom", "rep")),
        ),
        out_specs=(lead, lead, share, share, lead),
        check_vma=False,
    )
```

```python
import functools

import jax
import jax.numpy as jnp
from jax import lax
from jax.experimental import pallas as pl
from jax.experimental.pallas import tpu as pltpu
from jax.sharding import PartitionSpec as P

PTS = 512
N = 128
F32, BF16 = jnp.float32, jnp.bfloat16
MESH = pl.DeviceIdType.MESH
SWAP_AT = 4
PASS_AT = 7
TOPS_AT = 9
FORWARD_AT = 16
EARLY = 1
MAIN_VMEM = 54 << 20
LAST_VMEM = 1 << 20


def split3(x):
    high = x.astype(BF16)
    rest = x - high.astype(F32)
    mid = rest.astype(BF16)
    low = (rest - mid.astype(F32)).astype(BF16)
    return high, mid, low


def dot_tn(a, b):
    return lax.dot_general(a, b, (((0,), (0,)), ((), ())), preferred_element_type=F32)


def dot_nt(a, b):
    return lax.dot_general(a, b, (((1,), (1,)), ((), ())), preferred_element_type=F32)


def precise_tn(a, b):
    ah, am, al = split3(a)
    bh, bm, bl = split3(b)
    return dot_tn(
        jnp.concatenate([ah, ah, am, am, ah, al], 0),
        jnp.concatenate([bh, bm, bh, bm, bl, bh], 0),
    )


def precise_nn(a, b):
    return jnp.dot(a, b, precision=lax.Precision.HIGHEST, preferred_element_type=F32)


def precise_nt(a, b):
    return lax.dot_general(
        a, b, (((1,), (1,)), ((), ())), precision=lax.Precision.HIGHEST, preferred_element_type=F32
    )


def eliminate(m_ref, count, j):
    lane = lax.broadcasted_iota(jnp.int32, (1, 8, N), 2)
    sub = lax.broadcasted_iota(jnp.int32, (1, 8, N), 1)
    first = 8 * j
    rows = m_ref[:, first : first + 8, :]
    cols = [
        jnp.broadcast_to(rows[:, :, first + q : first + q + 1], (count, 8, N)) for q in range(8)
    ]
    inv = jnp.zeros((count, 8, N), F32)
    for q in range(8):
        r = 1.0 / cols[q][:, q : q + 1, :]
        inv = jnp.where(sub == q, r, inv)
        mult = jnp.where(sub > q, cols[q] * r, 0.0)
        for t in range(q + 1, 8):
            cols[t] = cols[t] - mult * cols[t][:, q : q + 1, :]
        rows = jnp.where(
            (lane == first + q) & (sub > q), -mult, rows - mult * rows[:, q : q + 1, :]
        )
    scale = jnp.sqrt(inv)
    done = rows * scale
    m_ref[:, first : first + 8, :] = done
    start = first + 8
    if start < N:
        row = first + sub
        ext = jnp.where(lane == row, scale, jnp.where((lane > row) & (lane < start), 0.0, done))
        lanes = lax.broadcasted_iota(jnp.int32, (N - start, N), 1)
        drop = (lanes >= first) & (lanes < start)
        for m in range(count):
            update = precise_tn(done[m], ext[m])[start:]
            m_ref[m, start:, :] = jnp.where(drop, 0.0, m_ref[m, start:, :]) - update


def upper(x):
    r = lax.broadcasted_iota(jnp.int32, (N, N), 0)
    c = lax.broadcasted_iota(jnp.int32, (N, N), 1)
    return jnp.where(c >= r, x, 0.0)


def lower_inverse(x):
    r = lax.broadcasted_iota(jnp.int32, (N, N), 0)
    c = lax.broadcasted_iota(jnp.int32, (N, N), 1)
    return jnp.where(c < r, x, jnp.where(c == r, 1.0 / x, 0.0))


def pack(ups):
    strips, halves = [], []
    for u in ups:
        strips.append(u[0:16])
        for i in (1, 2, 3):
            low = u[128 - 16 * i : 144 - 16 * i]
            strips.append(u[16 * i : 16 * i + 16] + pltpu.roll(low, 16 * i, 1))
        halves.append(u[64:80])
    for m in range(0, len(halves) - 1, 2):
        strips.append(halves[m] + pltpu.roll(halves[m + 1], 64, 1))
    if len(halves) % 2:
        strips.append(halves[-1])
    return strips


def main_kernel(
    n_leaf,
    row_ref, col_ref, leaf_hbm, trans_hbm, top_hbm, parts_hbm,
    orth_hbm, new_hbm, ntop_hbm, ftop_hbm, coup_hbm,
    leaf_v, trans_v, top_v, mats, tops, c2, a_in, f_in, own, fwd, r_stack, pool,
    orth_v, new_v, ntop_v, ftop_v, half_v, coup_v,
    in_sem, rs_send, rs_recv, g_send, g_recv, h_send, h_recv, out_sem, hello,
):
    leaf, dom, rep = lax.axis_index("leaf"), lax.axis_index("dom"), lax.axis_index("rep")
    lin = (leaf * 2 + dom) * 4 + rep
    total = n_leaf * 8

    def linear(shift):
        t = lax.rem(lin + shift + total, total)
        return (lax.div(t, 8), lax.rem(lax.div(t, 4), 2), lax.rem(t, 4))

    def ring(shift):
        return lax.rem(rep + shift, 4)

    def ring_id(shift):
        return (leaf, dom, ring(shift))

    def load(src, dst, k):
        copy = pltpu.make_async_copy(src, dst, in_sem.at[k])
        copy.start()
        return copy

    barrier = pltpu.get_barrier_semaphore()
    for target in (ring_id(1), ring_id(3)):
        pl.semaphore_signal(barrier, inc=1, device_id=target, device_id_type=MESH)

    @pl.when(rep == 0)
    def _():
        pl.semaphore_signal(barrier, inc=1, device_id=linear(-1), device_id_type=MESH)

    load_leaf = load(leaf_hbm, leaf_v, 0)
    load_trans = load(trans_hbm, trans_v, 1)
    load_top = load(top_hbm, top_v, 2)
    load_own = load(parts_hbm.at[0, pl.ds(16 * rep, 16)], own, 3)
    load_fr = load(parts_hbm.at[0, pl.ds(16 * ring(1), 8)], fwd.at[0], 4)
    load_fl = load(parts_hbm.at[0, pl.ds(16 * ring(3) + 8, 8)], fwd.at[1], 5)

    def lifted(g, e):
        return precise_tn(e, precise_tn(g, e))

    def leaf_grams():
        load_leaf.wait()
        for i in range(4):
            u = leaf_v[i]
            mats[i] = dot_tn(u, u) * (1.0 / PTS)
        load_trans.wait()

    def first_level():
        for p in range(2):
            mats[4 + p] = lifted(mats[2 * p], trans_v[2 * p]) + lifted(
                mats[2 * p + 1], trans_v[2 * p + 1]
            )

    def second_level():
        mats[6] = lifted(mats[4], trans_v[4]) + lifted(mats[5], trans_v[5])
        c2[0] = lifted(mats[6], trans_v[6])

    grams = [leaf_grams, first_level, second_level]
    for g in grams[:EARLY]:
        g()
    pl.semaphore_wait(barrier, 2 + lax.div(rep, 3))

    @pl.when(rep == 3)
    def _():
        pl.semaphore_signal(hello, inc=1, device_id=linear(1), device_id_type=MESH)

    def remote(src, dst, send, recv, target):
        copy = pltpu.make_async_remote_copy(
            src_ref=src, dst_ref=dst, send_sem=send, recv_sem=recv,
            device_id=target, device_id_type=MESH,
        )
        copy.start()
        return copy

    def block(dest, half):
        return parts_hbm.at[0, pl.ds(16 * ring(dest) + 8 * half, 8)]

    ar = remote(block(2, 0), a_in.at[0], rs_send.at[0], rs_recv.at[0], ring_id(1))
    al = remote(block(2, 1), a_in.at[1], rs_send.at[1], rs_recv.at[1], ring_id(3))

    for g in grams[EARLY:]:
        g()
    low_bit = lax.rem(rep, 2)
    swaps = [
        remote(c2.at[0], c2.at[1], g_send.at[0], g_recv.at[0], (leaf, dom, rep + 1 - 2 * low_bit))
    ]
    direct = []

    def send_direct():
        for part in range(2):
            for side, (dest, first, k) in enumerate(((1, 8, 2), (3, 0, 3))):
                rows = pl.ds(first + 4 * part, 4)
                k += 4 * part
                direct.append(
                    remote(
                        parts_hbm.at[0, pl.ds(16 * ring(dest) + first + 4 * part, 4)],
                        f_in.at[side, rows], rs_send.at[k], rs_recv.at[k], ring_id(dest),
                    )
                )

    second = []

    def swap_pairs():
        swaps[0].wait_recv()
        c2[2] = c2[0] + c2[1]
        swaps.append(
            remote(c2.at[2], c2.at[3], g_send.at[1], g_recv.at[1], (leaf, dom, 3 - rep))
        )

    def pass_on():
        ar.wait_recv()
        load_fr.wait()
        for i in range(8):
            fwd[0, i] = (fwd[0, i].astype(F32) + a_in[0, i].astype(F32)).astype(BF16)
        second.append(
            remote(fwd.at[0], f_in.at[0, pl.ds(0, 8)], rs_send.at[4], rs_recv.at[4], ring_id(1))
        )
        al.wait_recv()
        load_fl.wait()
        for i in range(8):
            fwd[1, i] = (fwd[1, i].astype(F32) + a_in[1, i].astype(F32)).astype(BF16)
        second.append(
            remote(fwd.at[1], f_in.at[1, pl.ds(8, 8)], rs_send.at[5], rs_recv.at[5], ring_id(3))
        )

    first_half = rep < 2

    def top_grams():
        swaps[1].wait_recv()
        load_top.wait()
        first_node = jnp.where(first_half, c2[2], c2[3])
        second_node = jnp.where(first_half, c2[3], c2[2])
        tops[0] = first_node
        tops[1] = second_node
        tops[2] = lifted(first_node, top_v[0]) + lifted(second_node, top_v[1])

    for j in range(N // 8):
        if j == SWAP_AT:
            swap_pairs()
        if j == PASS_AT:
            pass_on()
        if j == TOPS_AT:
            top_grams()
        eliminate(mats, 7, j)
        if j >= TOPS_AT:
            eliminate(tops, 3, j - TOPS_AT)

    ups = [upper(mats[i]) for i in range(7)]
    for i, strip in enumerate(pack(ups)):
        pool[2, i] = strip.astype(BF16)

    @pl.when(rep == 0)
    def _():
        pl.semaphore_wait(hello, 1)

    halo = [
        remote(pool.at[2], pool.at[1 + 2 * i], h_send.at[i], h_recv.at[i], linear(shift))
        for i, shift in enumerate((1, -1))
    ]
    send_direct()
    for i in range(7):
        r_stack[i] = ups[i].astype(BF16)

    def store(src, dst, k):
        copy = pltpu.make_async_copy(src, dst, out_sem.at[k])
        copy.start()
        return copy

    stores = []

    def forward():
        for i, shift in enumerate((1, -1)):
            halo[i].wait_recv()
            halo.append(
                remote(pool.at[1 + 2 * i], pool.at[4 * i], h_send.at[2 + i], h_recv.at[2 + i], linear(shift))
            )

    def halve(i):
        total_i = own[i].astype(F32) + (f_in[0, i].astype(F32) + f_in[1, i].astype(F32))
        return jnp.dot(
            r_stack[row_ref[i]], total_i.astype(BF16), preferred_element_type=F32
        ).astype(BF16)

    def project():
        load_own.wait()
        for s in [*second, *direct]:
            s.wait_recv()
        for i in range(16):
            half_v[i] = halve(i)
        for h in halo[2:]:
            h.wait_recv()
        lane = lax.broadcasted_iota(jnp.int32, (16, N), 1)

        def keep_from(x, first):
            return jnp.where(lane >= first, x, 0.0)

        for k in range(16):
            node = jnp.minimum(jnp.maximum(col_ref[k] - 7 * lin + 14, 0), 34)
            place = sum(jnp.where(node >= 7 * d, 1, 0) for d in (1, 2, 3, 4))
            slot = node - 7 * place
            half_slot = sum(jnp.where(slot >= d, 1, 0) for d in (2, 4, 6))
            strip = [pool[place, 4 * slot + i].astype(F32) for i in range(4)]
            pair = pool[place, 28 + half_slot].astype(F32)
            pair = jnp.where(slot - 2 * half_slot == 1, pltpu.roll(pair, 64, 1), pair)
            right = jnp.concatenate(
                [strip[0]]
                + [keep_from(strip[i], 16 * i) for i in (1, 2, 3)]
                + [keep_from(pair, 64)]
                + [keep_from(pltpu.roll(strip[i], N - 16 * i, 1), N - 16 * i) for i in (3, 2, 1)],
                0,
            ).astype(BF16)
            coup_v[k] = dot_nt(half_v[k], right).astype(BF16)
            if k % 8 == 7:
                part = pl.ds(k - 7, 8)
                stores.append(store(coup_v.at[part], coup_hbm.at[part], 5 + k // 8))

    for j in range(N // 8 - TOPS_AT, N // 8):
        if j == FORWARD_AT:
            forward()
        eliminate(tops, 3, j)
    if FORWARD_AT == 16:
        forward()

    for i in range(4):
        orth_v[i] = dot_nt(leaf_v[i], lower_inverse(mats[i]).astype(BF16)).astype(BF16)
    stores.append(store(orth_v, orth_hbm, 1))
    for c in range(6):
        inverse = lower_inverse(mats[4 + c // 2])
        new_v[c] = precise_nt(precise_nn(upper(mats[c]), trans_v[c]), inverse)
    own_three = jnp.where(first_half, tops[0], tops[1])
    new_v[6] = precise_nt(precise_nn(upper(mats[6]), trans_v[6]), lower_inverse(own_three))
    stores.append(store(new_v, new_hbm, 2))
    top_inverse = lower_inverse(tops[2])
    share = pl.ds(pl.multiple_of(rep * 32, 32), 32)
    row = lax.broadcasted_iota(jnp.int32, (32, N), 0) + rep * 32
    col = lax.broadcasted_iota(jnp.int32, (32, N), 1)
    keep = col >= row
    for t in range(2):
        part = jnp.where(keep, tops[t, share, :], 0.0)
        ntop_v[t] = precise_nt(precise_nn(part, top_v[t]), top_inverse)
    ftop_v[0] = jnp.where(keep, tops[2, share, :], 0.0)
    stores.append(store(ntop_v, ntop_hbm, 3))
    stores.append(store(ftop_v, ftop_hbm, 4))

    project()
    for copy in [ar, al, *direct, *swaps, *second, *halo]:
        copy.wait_send()
    for copy in stores:
        copy.wait()


def last_kernel(*refs):
    ins, outs, sems = refs[:5], refs[5:10], refs[10]
    copies = [pltpu.make_async_copy(a, b, sems.at[i]) for i, (a, b) in enumerate(zip(ins, outs))]
    for c in copies:
        c.start()
    for c in copies:
        c.wait()


def per_device(n_leaf, leaf_basis, transfer, transfer_top, coupling_parts, row_slot, col_node):
    any_ = pl.BlockSpec(memory_space=pl.ANY)
    smem = pl.BlockSpec(memory_space=pltpu.SMEM)
    shape = jax.ShapeDtypeStruct
    dma = pltpu.SemaphoreType.DMA
    results = [
        shape((4, PTS, N), BF16),
        shape((7, N, N), F32),
        shape((2, 32, N), F32),
        shape((1, 32, N), F32),
        shape((16, N, N), BF16),
    ]
    outs = pl.pallas_call(
        functools.partial(main_kernel, n_leaf),
        out_shape=[pltpu.VMEM(r.shape, r.dtype) for r in results],
        in_specs=[smem] * 2 + [any_] * 4,
        out_specs=[any_] * 5,
        scratch_shapes=[
            pltpu.VMEM((4, PTS, N), BF16),
            pltpu.VMEM((7, N, N), F32),
            pltpu.VMEM((2, N, N), F32),
            pltpu.VMEM((7, N, N), F32),
            pltpu.VMEM((3, N, N), F32),
            pltpu.VMEM((4, N, N), F32),
            pltpu.VMEM((2, 8, N, N), BF16),
            pltpu.VMEM((2, 16, N, N), BF16),
            pltpu.VMEM((16, N, N), BF16),
            pltpu.VMEM((2, 8, N, N), BF16),
            pltpu.VMEM((7, N, N), BF16),
            pltpu.VMEM((5, 32, 16, N), BF16),
            pltpu.VMEM((4, PTS, N), BF16),
            pltpu.VMEM((7, N, N), F32),
            pltpu.VMEM((2, 32, N), F32),
            pltpu.VMEM((1, 32, N), F32),
            pltpu.VMEM((16, N, N), BF16),
            pltpu.VMEM((16, N, N), BF16),
            dma((6,)), dma((8,)), dma((8,)), dma((2,)), dma((2,)), dma((4,)), dma((4,)), dma((7,)),
            pltpu.SemaphoreType.REGULAR,
        ],
        compiler_params=pltpu.CompilerParams(
            collective_id=0, has_side_effects=True, vmem_limit_bytes=MAIN_VMEM
        ),
        name="factor_and_send",
    )(row_slot, col_node, leaf_basis, transfer, transfer_top, coupling_parts)
    return pl.pallas_call(
        last_kernel,
        out_shape=results,
        in_specs=[any_] * 5,
        out_specs=[any_] * 5,
        scratch_shapes=[dma((5,))],
        compiler_params=pltpu.CompilerParams(vmem_limit_bytes=LAST_VMEM),
        name="hand_over",
    )(*outs)


def solution(mesh):
    lead = P(("leaf", "dom", "rep"), None, None)
    share = P(("leaf", "dom"), "rep", None)
    return jax.shard_map(
        functools.partial(per_device, mesh.shape["leaf"]),
        mesh=mesh,
        in_specs=(
            lead,
            lead,
            P(("leaf", "dom"), None, None),
            P("rep", ("leaf", "dom"), None, None),
            P(("leaf", "dom", "rep")),
            P(("leaf", "dom", "rep")),
        ),
        out_specs=(lead, lead, share, share, lead),
        check_vma=False,
    )
```

```python
import functools

import jax
import jax.numpy as jnp
from jax import lax
from jax.experimental import pallas as pl
from jax.experimental.pallas import tpu as pltpu
from jax.sharding import PartitionSpec as P

PTS = 512
N = 128
F32, BF16 = jnp.float32, jnp.bfloat16
MESH = pl.DeviceIdType.MESH
SWAP_AT = 4
PASS_AT = 7
TOPS_AT = 15
FORWARD_AT = 9
EARLY = 1
MAIN_VMEM = 54 << 20
LAST_VMEM = 1 << 20


def split3(x):
    high = x.astype(BF16)
    rest = x - high.astype(F32)
    mid = rest.astype(BF16)
    low = (rest - mid.astype(F32)).astype(BF16)
    return high, mid, low


def dot_tn(a, b):
    return lax.dot_general(a, b, (((0,), (0,)), ((), ())), preferred_element_type=F32)


def dot_nt(a, b):
    return lax.dot_general(a, b, (((1,), (1,)), ((), ())), preferred_element_type=F32)


def precise_tn(a, b):
    ah, am, al = split3(a)
    bh, bm, bl = split3(b)
    return dot_tn(
        jnp.concatenate([ah, ah, am, am, ah, al], 0),
        jnp.concatenate([bh, bm, bh, bm, bl, bh], 0),
    )


def precise_nn(a, b):
    return jnp.dot(a, b, precision=lax.Precision.HIGHEST, preferred_element_type=F32)


def precise_nt(a, b):
    return lax.dot_general(
        a, b, (((1,), (1,)), ((), ())), precision=lax.Precision.HIGHEST, preferred_element_type=F32
    )


def eliminate(m_ref, count, j):
    lane = lax.broadcasted_iota(jnp.int32, (1, 8, N), 2)
    sub = lax.broadcasted_iota(jnp.int32, (1, 8, N), 1)
    first = 8 * j
    rows = m_ref[:, first : first + 8, :]
    cols = [
        jnp.broadcast_to(rows[:, :, first + q : first + q + 1], (count, 8, N)) for q in range(8)
    ]
    inv = jnp.zeros((count, 8, N), F32)
    for q in range(8):
        r = 1.0 / cols[q][:, q : q + 1, :]
        inv = jnp.where(sub == q, r, inv)
        mult = jnp.where(sub > q, cols[q] * r, 0.0)
        for t in range(q + 1, 8):
            cols[t] = cols[t] - mult * cols[t][:, q : q + 1, :]
        rows = jnp.where(
            (lane == first + q) & (sub > q), -mult, rows - mult * rows[:, q : q + 1, :]
        )
    scale = jnp.sqrt(inv)
    done = rows * scale
    m_ref[:, first : first + 8, :] = done
    start = first + 8
    if start < N:
        row = first + sub
        ext = jnp.where(lane == row, scale, jnp.where((lane > row) & (lane < start), 0.0, done))
        lanes = lax.broadcasted_iota(jnp.int32, (N - start, N), 1)
        drop = (lanes >= first) & (lanes < start)
        for m in range(count):
            update = precise_tn(done[m], ext[m])[start:]
            m_ref[m, start:, :] = jnp.where(drop, 0.0, m_ref[m, start:, :]) - update


def upper(x):
    r = lax.broadcasted_iota(jnp.int32, (N, N), 0)
    c = lax.broadcasted_iota(jnp.int32, (N, N), 1)
    return jnp.where(c >= r, x, 0.0)


def lower_inverse(x):
    r = lax.broadcasted_iota(jnp.int32, (N, N), 0)
    c = lax.broadcasted_iota(jnp.int32, (N, N), 1)
    return jnp.where(c < r, x, jnp.where(c == r, 1.0 / x, 0.0))


def pack(ups):
    strips, halves = [], []
    for u in ups:
        strips.append(u[0:16])
        for i in (1, 2, 3):
            low = u[128 - 16 * i : 144 - 16 * i]
            strips.append(u[16 * i : 16 * i + 16] + pltpu.roll(low, 16 * i, 1))
        halves.append(u[64:80])
    for m in range(0, len(halves) - 1, 2):
        strips.append(halves[m] + pltpu.roll(halves[m + 1], 64, 1))
    if len(halves) % 2:
        strips.append(halves[-1])
    return strips


def main_kernel(
    n_leaf,
    row_ref, col_ref, leaf_hbm, trans_hbm, top_hbm, parts_hbm,
    orth_hbm, new_hbm, ntop_hbm, ftop_hbm, coup_hbm,
    leaf_v, trans_v, top_v, mats, tops, c2, a_in, f_in, own, fwd, r_stack, pool,
    orth_v, new_v, ntop_v, ftop_v, half_v, coup_v,
    in_sem, rs_send, rs_recv, g_send, g_recv, h_send, h_recv, out_sem, hello,
):
    leaf, dom, rep = lax.axis_index("leaf"), lax.axis_index("dom"), lax.axis_index("rep")
    lin = (leaf * 2 + dom) * 4 + rep
    total = n_leaf * 8

    def linear(shift):
        t = lax.rem(lin + shift + total, total)
        return (lax.div(t, 8), lax.rem(lax.div(t, 4), 2), lax.rem(t, 4))

    def ring(shift):
        return lax.rem(rep + shift, 4)

    def ring_id(shift):
        return (leaf, dom, ring(shift))

    def load(src, dst, k):
        copy = pltpu.make_async_copy(src, dst, in_sem.at[k])
        copy.start()
        return copy

    barrier = pltpu.get_barrier_semaphore()
    for target in (ring_id(1), ring_id(3)):
        pl.semaphore_signal(barrier, inc=1, device_id=target, device_id_type=MESH)

    @pl.when(rep == 0)
    def _():
        pl.semaphore_signal(barrier, inc=1, device_id=linear(-1), device_id_type=MESH)

    load_leaf = load(leaf_hbm, leaf_v, 0)
    load_trans = load(trans_hbm, trans_v, 1)
    load_top = load(top_hbm, top_v, 2)
    load_own = load(parts_hbm.at[0, pl.ds(16 * rep, 16)], own, 3)
    load_fr = load(parts_hbm.at[0, pl.ds(16 * ring(1), 8)], fwd.at[0], 4)
    load_fl = load(parts_hbm.at[0, pl.ds(16 * ring(3) + 8, 8)], fwd.at[1], 5)

    def lifted(g, e):
        return precise_tn(e, precise_tn(g, e))

    def leaf_grams():
        load_leaf.wait()
        for i in range(4):
            u = leaf_v[i]
            mats[i] = dot_tn(u, u) * (1.0 / PTS)
        load_trans.wait()

    def first_level():
        for p in range(2):
            mats[4 + p] = lifted(mats[2 * p], trans_v[2 * p]) + lifted(
                mats[2 * p + 1], trans_v[2 * p + 1]
            )

    def second_level():
        mats[6] = lifted(mats[4], trans_v[4]) + lifted(mats[5], trans_v[5])
        c2[0] = lifted(mats[6], trans_v[6])

    grams = [leaf_grams, first_level, second_level]
    for g in grams[:EARLY]:
        g()
    pl.semaphore_wait(barrier, 2 + lax.div(rep, 3))

    @pl.when(rep == 3)
    def _():
        pl.semaphore_signal(hello, inc=1, device_id=linear(1), device_id_type=MESH)

    def remote(src, dst, send, recv, target):
        copy = pltpu.make_async_remote_copy(
            src_ref=src, dst_ref=dst, send_sem=send, recv_sem=recv,
            device_id=target, device_id_type=MESH,
        )
        copy.start()
        return copy

    def block(dest, half):
        return parts_hbm.at[0, pl.ds(16 * ring(dest) + 8 * half, 8)]

    ar = remote(block(2, 0), a_in.at[0], rs_send.at[0], rs_recv.at[0], ring_id(1))
    al = remote(block(2, 1), a_in.at[1], rs_send.at[1], rs_recv.at[1], ring_id(3))

    for g in grams[EARLY:]:
        g()
    low_bit = lax.rem(rep, 2)
    swaps = [
        remote(c2.at[0], c2.at[1], g_send.at[0], g_recv.at[0], (leaf, dom, rep + 1 - 2 * low_bit))
    ]
    direct = []

    def send_direct():
        for part in range(2):
            for side, (dest, first, k) in enumerate(((1, 8, 2), (3, 0, 3))):
                rows = pl.ds(first + 4 * part, 4)
                k += 4 * part
                direct.append(
                    remote(
                        parts_hbm.at[0, pl.ds(16 * ring(dest) + first + 4 * part, 4)],
                        f_in.at[side, rows], rs_send.at[k], rs_recv.at[k], ring_id(dest),
                    )
                )

    second = []

    def swap_pairs():
        swaps[0].wait_recv()
        c2[2] = c2[0] + c2[1]
        swaps.append(
            remote(c2.at[2], c2.at[3], g_send.at[1], g_recv.at[1], (leaf, dom, 3 - rep))
        )

    def pass_on():
        ar.wait_recv()
        load_fr.wait()
        for i in range(8):
            fwd[0, i] = (fwd[0, i].astype(F32) + a_in[0, i].astype(F32)).astype(BF16)
        second.append(
            remote(fwd.at[0], f_in.at[0, pl.ds(0, 8)], rs_send.at[4], rs_recv.at[4], ring_id(1))
        )
        al.wait_recv()
        load_fl.wait()
        for i in range(8):
            fwd[1, i] = (fwd[1, i].astype(F32) + a_in[1, i].astype(F32)).astype(BF16)
        second.append(
            remote(fwd.at[1], f_in.at[1, pl.ds(8, 8)], rs_send.at[5], rs_recv.at[5], ring_id(3))
        )

    first_half = rep < 2

    def top_grams():
        swaps[1].wait_recv()
        load_top.wait()
        first_node = jnp.where(first_half, c2[2], c2[3])
        second_node = jnp.where(first_half, c2[3], c2[2])
        tops[0] = first_node
        tops[1] = second_node
        tops[2] = lifted(first_node, top_v[0]) + lifted(second_node, top_v[1])

    for j in range(N // 8):
        if j == SWAP_AT:
            swap_pairs()
        if j == PASS_AT:
            pass_on()
        if j == TOPS_AT:
            top_grams()
        eliminate(mats, 7, j)
        if j >= TOPS_AT:
            eliminate(tops, 3, j - TOPS_AT)

    ups = [upper(mats[i]) for i in range(7)]
    for i, strip in enumerate(pack(ups)):
        pool[2, i] = strip.astype(BF16)

    @pl.when(rep == 0)
    def _():
        pl.semaphore_wait(hello, 1)

    halo = [
        remote(pool.at[2], pool.at[1 + 2 * i], h_send.at[i], h_recv.at[i], linear(shift))
        for i, shift in enumerate((1, -1))
    ]
    send_direct()
    for i in range(7):
        r_stack[i] = ups[i].astype(BF16)

    def store(src, dst, k):
        copy = pltpu.make_async_copy(src, dst, out_sem.at[k])
        copy.start()
        return copy

    stores = []

    def forward():
        for i, shift in enumerate((1, -1)):
            halo[i].wait_recv()
            halo.append(
                remote(pool.at[1 + 2 * i], pool.at[4 * i], h_send.at[2 + i], h_recv.at[2 + i], linear(shift))
            )

    def halve(i):
        total_i = own[i].astype(F32) + (f_in[0, i].astype(F32) + f_in[1, i].astype(F32))
        return jnp.dot(
            r_stack[row_ref[i]], total_i.astype(BF16), preferred_element_type=F32
        ).astype(BF16)

    def project():
        load_own.wait()
        for s in [*second, *direct]:
            s.wait_recv()
        for i in range(16):
            half_v[i] = halve(i)
        for h in halo[2:]:
            h.wait_recv()
        lane = lax.broadcasted_iota(jnp.int32, (16, N), 1)

        def keep_from(x, first):
            return jnp.where(lane >= first, x, 0.0)

        for k in range(16):
            node = jnp.minimum(jnp.maximum(col_ref[k] - 7 * lin + 14, 0), 34)
            place = sum(jnp.where(node >= 7 * d, 1, 0) for d in (1, 2, 3, 4))
            slot = node - 7 * place
            half_slot = sum(jnp.where(slot >= d, 1, 0) for d in (2, 4, 6))
            strip = [pool[place, 4 * slot + i].astype(F32) for i in range(4)]
            pair = pool[place, 28 + half_slot].astype(F32)
            pair = jnp.where(slot - 2 * half_slot == 1, pltpu.roll(pair, 64, 1), pair)
            right = jnp.concatenate(
                [strip[0]]
                + [keep_from(strip[i], 16 * i) for i in (1, 2, 3)]
                + [keep_from(pair, 64)]
                + [keep_from(pltpu.roll(strip[i], N - 16 * i, 1), N - 16 * i) for i in (3, 2, 1)],
                0,
            ).astype(BF16)
            coup_v[k] = dot_nt(half_v[k], right).astype(BF16)
            if k % 8 == 7:
                part = pl.ds(k - 7, 8)
                stores.append(store(coup_v.at[part], coup_hbm.at[part], 5 + k // 8))

    for j in range(N // 8 - TOPS_AT, N // 8):
        if j == FORWARD_AT:
            forward()
        eliminate(tops, 3, j)
    if FORWARD_AT == 16:
        forward()

    for i in range(4):
        orth_v[i] = dot_nt(leaf_v[i], lower_inverse(mats[i]).astype(BF16)).astype(BF16)
    stores.append(store(orth_v, orth_hbm, 1))
    for c in range(6):
        inverse = lower_inverse(mats[4 + c // 2])
        new_v[c] = precise_nt(precise_nn(upper(mats[c]), trans_v[c]), inverse)
    own_three = jnp.where(first_half, tops[0], tops[1])
    new_v[6] = precise_nt(precise_nn(upper(mats[6]), trans_v[6]), lower_inverse(own_three))
    stores.append(store(new_v, new_hbm, 2))
    top_inverse = lower_inverse(tops[2])
    share = pl.ds(pl.multiple_of(rep * 32, 32), 32)
    row = lax.broadcasted_iota(jnp.int32, (32, N), 0) + rep * 32
    col = lax.broadcasted_iota(jnp.int32, (32, N), 1)
    keep = col >= row
    for t in range(2):
        part = jnp.where(keep, tops[t, share, :], 0.0)
        ntop_v[t] = precise_nt(precise_nn(part, top_v[t]), top_inverse)
    ftop_v[0] = jnp.where(keep, tops[2, share, :], 0.0)
    stores.append(store(ntop_v, ntop_hbm, 3))
    stores.append(store(ftop_v, ftop_hbm, 4))

    project()
    for copy in [ar, al, *direct, *swaps, *second, *halo]:
        copy.wait_send()
    for copy in stores:
        copy.wait()


def last_kernel(*refs):
    ins, outs, sems = refs[:5], refs[5:10], refs[10]
    copies = [pltpu.make_async_copy(a, b, sems.at[i]) for i, (a, b) in enumerate(zip(ins, outs))]
    for c in copies:
        c.start()
    for c in copies:
        c.wait()


def per_device(n_leaf, leaf_basis, transfer, transfer_top, coupling_parts, row_slot, col_node):
    any_ = pl.BlockSpec(memory_space=pl.ANY)
    smem = pl.BlockSpec(memory_space=pltpu.SMEM)
    shape = jax.ShapeDtypeStruct
    dma = pltpu.SemaphoreType.DMA
    results = [
        shape((4, PTS, N), BF16),
        shape((7, N, N), F32),
        shape((2, 32, N), F32),
        shape((1, 32, N), F32),
        shape((16, N, N), BF16),
    ]
    outs = pl.pallas_call(
        functools.partial(main_kernel, n_leaf),
        out_shape=[pltpu.VMEM(r.shape, r.dtype) for r in results],
        in_specs=[smem] * 2 + [any_] * 4,
        out_specs=[any_] * 5,
        scratch_shapes=[
            pltpu.VMEM((4, PTS, N), BF16),
            pltpu.VMEM((7, N, N), F32),
            pltpu.VMEM((2, N, N), F32),
            pltpu.VMEM((7, N, N), F32),
            pltpu.VMEM((3, N, N), F32),
            pltpu.VMEM((4, N, N), F32),
            pltpu.VMEM((2, 8, N, N), BF16),
            pltpu.VMEM((2, 16, N, N), BF16),
            pltpu.VMEM((16, N, N), BF16),
            pltpu.VMEM((2, 8, N, N), BF16),
            pltpu.VMEM((7, N, N), BF16),
            pltpu.VMEM((5, 32, 16, N), BF16),
            pltpu.VMEM((4, PTS, N), BF16),
            pltpu.VMEM((7, N, N), F32),
            pltpu.VMEM((2, 32, N), F32),
            pltpu.VMEM((1, 32, N), F32),
            pltpu.VMEM((16, N, N), BF16),
            pltpu.VMEM((16, N, N), BF16),
            dma((6,)), dma((8,)), dma((8,)), dma((2,)), dma((2,)), dma((4,)), dma((4,)), dma((7,)),
            pltpu.SemaphoreType.REGULAR,
        ],
        compiler_params=pltpu.CompilerParams(
            collective_id=0, has_side_effects=True, vmem_limit_bytes=MAIN_VMEM
        ),
        name="factor_and_send",
    )(row_slot, col_node, leaf_basis, transfer, transfer_top, coupling_parts)
    return pl.pallas_call(
        last_kernel,
        out_shape=results,
        in_specs=[any_] * 5,
        out_specs=[any_] * 5,
        scratch_shapes=[dma((5,))],
        compiler_params=pltpu.CompilerParams(vmem_limit_bytes=LAST_VMEM),
        name="hand_over",
    )(*outs)


def solution(mesh):
    lead = P(("leaf", "dom", "rep"), None, None)
    share = P(("leaf", "dom"), "rep", None)
    return jax.shard_map(
        functools.partial(per_device, mesh.shape["leaf"]),
        mesh=mesh,
        in_specs=(
            lead,
            lead,
            P(("leaf", "dom"), None, None),
            P("rep", ("leaf", "dom"), None, None),
            P(("leaf", "dom", "rep")),
            P(("leaf", "dom", "rep")),
        ),
        out_specs=(lead, lead, share, share, lead),
        check_vma=False,
    )
```

```python
import functools

import jax
import jax.numpy as jnp
from jax import lax
from jax.experimental import pallas as pl
from jax.experimental.pallas import tpu as pltpu
from jax.sharding import PartitionSpec as P

PTS = 512
N = 128
F32, BF16 = jnp.float32, jnp.bfloat16
MESH = pl.DeviceIdType.MESH
SWAP_AT = 4
PASS_AT = 7
TOPS_AT = 15
FORWARD_AT = 9
EARLY = 1
MAIN_VMEM = 54 << 20
LAST_VMEM = 1 << 20


def split3(x):
    high = x.astype(BF16)
    rest = x - high.astype(F32)
    mid = rest.astype(BF16)
    low = (rest - mid.astype(F32)).astype(BF16)
    return high, mid, low


def dot_tn(a, b):
    return lax.dot_general(a, b, (((0,), (0,)), ((), ())), preferred_element_type=F32)


def dot_nt(a, b):
    return lax.dot_general(a, b, (((1,), (1,)), ((), ())), preferred_element_type=F32)


def precise_tn(a, b):
    ah, am, al = split3(a)
    bh, bm, bl = split3(b)
    return dot_tn(
        jnp.concatenate([ah, ah, am, am, ah, al], 0),
        jnp.concatenate([bh, bm, bh, bm, bl, bh], 0),
    )


def precise_nn(a, b):
    return jnp.dot(a, b, precision=lax.Precision.HIGHEST, preferred_element_type=F32)


def precise_nt(a, b):
    return lax.dot_general(
        a, b, (((1,), (1,)), ((), ())), precision=lax.Precision.HIGHEST, preferred_element_type=F32
    )


def eliminate(m_ref, count, j):
    lane = lax.broadcasted_iota(jnp.int32, (1, 8, N), 2)
    sub = lax.broadcasted_iota(jnp.int32, (1, 8, N), 1)
    first = 8 * j
    rows = m_ref[:, first : first + 8, :]
    cols = [
        jnp.broadcast_to(rows[:, :, first + q : first + q + 1], (count, 8, N)) for q in range(8)
    ]
    inv = jnp.zeros((count, 8, N), F32)
    for q in range(8):
        r = 1.0 / cols[q][:, q : q + 1, :]
        inv = jnp.where(sub == q, r, inv)
        mult = jnp.where(sub > q, cols[q] * r, 0.0)
        for t in range(q + 1, 8):
            cols[t] = cols[t] - mult * cols[t][:, q : q + 1, :]
        rows = jnp.where(
            (lane == first + q) & (sub > q), -mult, rows - mult * rows[:, q : q + 1, :]
        )
    scale = jnp.sqrt(inv)
    done = rows * scale
    m_ref[:, first : first + 8, :] = done
    start = first + 8
    if start < N:
        row = first + sub
        ext = jnp.where(lane == row, scale, jnp.where((lane > row) & (lane < start), 0.0, done))
        lanes = lax.broadcasted_iota(jnp.int32, (N - start, N), 1)
        drop = (lanes >= first) & (lanes < start)
        for m in range(count):
            update = precise_tn(done[m], ext[m])[start:]
            m_ref[m, start:, :] = jnp.where(drop, 0.0, m_ref[m, start:, :]) - update


def upper(x):
    r = lax.broadcasted_iota(jnp.int32, (N, N), 0)
    c = lax.broadcasted_iota(jnp.int32, (N, N), 1)
    return jnp.where(c >= r, x, 0.0)


def lower_inverse(x):
    r = lax.broadcasted_iota(jnp.int32, (N, N), 0)
    c = lax.broadcasted_iota(jnp.int32, (N, N), 1)
    return jnp.where(c < r, x, jnp.where(c == r, 1.0 / x, 0.0))


def pack(ups):
    strips, halves = [], []
    for u in ups:
        strips.append(u[0:16])
        for i in (1, 2, 3):
            low = u[128 - 16 * i : 144 - 16 * i]
            strips.append(u[16 * i : 16 * i + 16] + pltpu.roll(low, 16 * i, 1))
        halves.append(u[64:80])
    for m in range(0, len(halves) - 1, 2):
        strips.append(halves[m] + pltpu.roll(halves[m + 1], 64, 1))
    if len(halves) % 2:
        strips.append(halves[-1])
    return strips


def main_kernel(
    n_leaf,
    row_ref, col_ref, leaf_hbm, trans_hbm, top_hbm, parts_hbm,
    orth_hbm, new_hbm, ntop_hbm, ftop_hbm, coup_hbm,
    leaf_v, trans_v, top_v, mats, tops, c2, a_in, f_in, own, fwd, r_stack, pool,
    orth_v, new_v, ntop_v, ftop_v, half_v, coup_v,
    in_sem, rs_send, rs_recv, g_send, g_recv, h_send, h_recv, out_sem, hello,
):
    leaf, dom, rep = lax.axis_index("leaf"), lax.axis_index("dom"), lax.axis_index("rep")
    lin = (leaf * 2 + dom) * 4 + rep
    total = n_leaf * 8

    def linear(shift):
        t = lax.rem(lin + shift + total, total)
        return (lax.div(t, 8), lax.rem(lax.div(t, 4), 2), lax.rem(t, 4))

    def ring(shift):
        return lax.rem(rep + shift, 4)

    def ring_id(shift):
        return (leaf, dom, ring(shift))

    def load(src, dst, k):
        copy = pltpu.make_async_copy(src, dst, in_sem.at[k])
        copy.start()
        return copy

    barrier = pltpu.get_barrier_semaphore()
    for target in (ring_id(1), ring_id(3)):
        pl.semaphore_signal(barrier, inc=1, device_id=target, device_id_type=MESH)

    @pl.when(rep == 0)
    def _():
        pl.semaphore_signal(barrier, inc=1, device_id=linear(-1), device_id_type=MESH)

    load_leaf = load(leaf_hbm, leaf_v, 0)
    load_trans = load(trans_hbm, trans_v, 1)
    load_top = load(top_hbm, top_v, 2)
    load_own = load(parts_hbm.at[0, pl.ds(16 * rep, 16)], own, 3)
    load_fr = load(parts_hbm.at[0, pl.ds(16 * ring(1), 8)], fwd.at[0], 4)
    load_fl = load(parts_hbm.at[0, pl.ds(16 * ring(3) + 8, 8)], fwd.at[1], 5)

    def lifted(g, e):
        return precise_tn(e, precise_tn(g, e))

    def leaf_grams():
        load_leaf.wait()
        for i in range(4):
            u = leaf_v[i]
            mats[i] = dot_tn(u, u) * (1.0 / PTS)
        load_trans.wait()

    def first_level():
        for p in range(2):
            mats[4 + p] = lifted(mats[2 * p], trans_v[2 * p]) + lifted(
                mats[2 * p + 1], trans_v[2 * p + 1]
            )

    def second_level():
        mats[6] = lifted(mats[4], trans_v[4]) + lifted(mats[5], trans_v[5])
        c2[0] = lifted(mats[6], trans_v[6])

    grams = [leaf_grams, first_level, second_level]
    for g in grams[:EARLY]:
        g()
    pl.semaphore_wait(barrier, 2 + lax.div(rep, 3))

    @pl.when(rep == 3)
    def _():
        pl.semaphore_signal(hello, inc=1, device_id=linear(1), device_id_type=MESH)

    def remote(src, dst, send, recv, target):
        copy = pltpu.make_async_remote_copy(
            src_ref=src, dst_ref=dst, send_sem=send, recv_sem=recv,
            device_id=target, device_id_type=MESH,
        )
        copy.start()
        return copy

    def block(dest, half):
        return parts_hbm.at[0, pl.ds(16 * ring(dest) + 8 * half, 8)]

    ar = remote(block(2, 0), a_in.at[0], rs_send.at[0], rs_recv.at[0], ring_id(1))
    al = remote(block(2, 1), a_in.at[1], rs_send.at[1], rs_recv.at[1], ring_id(3))

    for g in grams[EARLY:]:
        g()
    low_bit = lax.rem(rep, 2)
    swaps = [
        remote(c2.at[0], c2.at[1], g_send.at[0], g_recv.at[0], (leaf, dom, rep + 1 - 2 * low_bit))
    ]
    direct = []

    def send_direct():
        for part in range(2):
            for side, (dest, first, k) in enumerate(((1, 8, 2), (3, 0, 3))):
                rows = pl.ds(first + 4 * part, 4)
                k += 4 * part
                direct.append(
                    remote(
                        parts_hbm.at[0, pl.ds(16 * ring(dest) + first + 4 * part, 4)],
                        f_in.at[side, rows], rs_send.at[k], rs_recv.at[k], ring_id(dest),
                    )
                )

    second = []

    def swap_pairs():
        swaps[0].wait_recv()
        c2[2] = c2[0] + c2[1]
        swaps.append(
            remote(c2.at[2], c2.at[3], g_send.at[1], g_recv.at[1], (leaf, dom, 3 - rep))
        )

    def pass_on():
        ar.wait_recv()
        load_fr.wait()
        for i in range(8):
            fwd[0, i] = (fwd[0, i].astype(F32) + a_in[0, i].astype(F32)).astype(BF16)
        second.append(
            remote(fwd.at[0], f_in.at[0, pl.ds(0, 8)], rs_send.at[4], rs_recv.at[4], ring_id(1))
        )
        al.wait_recv()
        load_fl.wait()
        for i in range(8):
            fwd[1, i] = (fwd[1, i].astype(F32) + a_in[1, i].astype(F32)).astype(BF16)
        second.append(
            remote(fwd.at[1], f_in.at[1, pl.ds(8, 8)], rs_send.at[5], rs_recv.at[5], ring_id(3))
        )

    first_half = rep < 2

    def top_grams():
        swaps[1].wait_recv()
        load_top.wait()
        first_node = jnp.where(first_half, c2[2], c2[3])
        second_node = jnp.where(first_half, c2[3], c2[2])
        tops[0] = first_node
        tops[1] = second_node
        tops[2] = lifted(first_node, top_v[0]) + lifted(second_node, top_v[1])

    for j in range(N // 8):
        if j == SWAP_AT:
            swap_pairs()
        if j == PASS_AT:
            pass_on()
        if j == TOPS_AT:
            top_grams()
        eliminate(mats, 7, j)
        if j >= TOPS_AT:
            eliminate(tops, 3, j - TOPS_AT)

    ups = [upper(mats[i]) for i in range(7)]
    for i, strip in enumerate(pack(ups)):
        pool[2, i] = strip.astype(BF16)

    @pl.when(rep == 0)
    def _():
        pl.semaphore_wait(hello, 1)

    halo = [
        remote(pool.at[2], pool.at[1 + 2 * i], h_send.at[i], h_recv.at[i], linear(shift))
        for i, shift in enumerate((1, -1))
    ]
    send_direct()
    for i in range(7):
        r_stack[i] = ups[i].astype(BF16)

    def store(src, dst, k):
        copy = pltpu.make_async_copy(src, dst, out_sem.at[k])
        copy.start()
        return copy

    stores = []

    def forward():
        for i, shift in enumerate((1, -1)):
            halo[i].wait_recv()
            halo.append(
                remote(pool.at[1 + 2 * i], pool.at[4 * i], h_send.at[2 + i], h_recv.at[2 + i], linear(shift))
            )

    def halve(i):
        total_i = own[i].astype(F32) + (f_in[0, i].astype(F32) + f_in[1, i].astype(F32))
        return jnp.dot(
            r_stack[row_ref[i]], total_i.astype(BF16), preferred_element_type=F32
        ).astype(BF16)

    def project():
        load_own.wait()
        for s in second:
            s.wait_recv()
        for part in range(2):
            for s in direct[2 * part : 2 * part + 2]:
                s.wait_recv()
            for i in [first + 4 * part + n for first in (0, 8) for n in range(4)]:
                half_v[i] = halve(i)
        for h in halo[2:]:
            h.wait_recv()
        lane = lax.broadcasted_iota(jnp.int32, (16, N), 1)

        def keep_from(x, first):
            return jnp.where(lane >= first, x, 0.0)

        for k in range(16):
            node = jnp.minimum(jnp.maximum(col_ref[k] - 7 * lin + 14, 0), 34)
            place = sum(jnp.where(node >= 7 * d, 1, 0) for d in (1, 2, 3, 4))
            slot = node - 7 * place
            half_slot = sum(jnp.where(slot >= d, 1, 0) for d in (2, 4, 6))
            strip = [pool[place, 4 * slot + i].astype(F32) for i in range(4)]
            pair = pool[place, 28 + half_slot].astype(F32)
            pair = jnp.where(slot - 2 * half_slot == 1, pltpu.roll(pair, 64, 1), pair)
            right = jnp.concatenate(
                [strip[0]]
                + [keep_from(strip[i], 16 * i) for i in (1, 2, 3)]
                + [keep_from(pair, 64)]
                + [keep_from(pltpu.roll(strip[i], N - 16 * i, 1), N - 16 * i) for i in (3, 2, 1)],
                0,
            ).astype(BF16)
            coup_v[k] = dot_nt(half_v[k], right).astype(BF16)
            if k % 8 == 7:
                part = pl.ds(k - 7, 8)
                stores.append(store(coup_v.at[part], coup_hbm.at[part], 5 + k // 8))

    for j in range(N // 8 - TOPS_AT, N // 8):
        if j == FORWARD_AT:
            forward()
        eliminate(tops, 3, j)
    if FORWARD_AT == 16:
        forward()

    for i in range(4):
        orth_v[i] = dot_nt(leaf_v[i], lower_inverse(mats[i]).astype(BF16)).astype(BF16)
    stores.append(store(orth_v, orth_hbm, 1))
    for c in range(6):
        inverse = lower_inverse(mats[4 + c // 2])
        new_v[c] = precise_nt(precise_nn(upper(mats[c]), trans_v[c]), inverse)
    own_three = jnp.where(first_half, tops[0], tops[1])
    new_v[6] = precise_nt(precise_nn(upper(mats[6]), trans_v[6]), lower_inverse(own_three))
    stores.append(store(new_v, new_hbm, 2))
    top_inverse = lower_inverse(tops[2])
    share = pl.ds(pl.multiple_of(rep * 32, 32), 32)
    row = lax.broadcasted_iota(jnp.int32, (32, N), 0) + rep * 32
    col = lax.broadcasted_iota(jnp.int32, (32, N), 1)
    keep = col >= row
    for t in range(2):
        part = jnp.where(keep, tops[t, share, :], 0.0)
        ntop_v[t] = precise_nt(precise_nn(part, top_v[t]), top_inverse)
    ftop_v[0] = jnp.where(keep, tops[2, share, :], 0.0)
    stores.append(store(ntop_v, ntop_hbm, 3))
    stores.append(store(ftop_v, ftop_hbm, 4))

    project()
    for copy in [ar, al, *direct, *swaps, *second, *halo]:
        copy.wait_send()
    for copy in stores:
        copy.wait()


def last_kernel(*refs):
    ins, outs, sems = refs[:5], refs[5:10], refs[10]
    copies = [pltpu.make_async_copy(a, b, sems.at[i]) for i, (a, b) in enumerate(zip(ins, outs))]
    for c in copies:
        c.start()
    for c in copies:
        c.wait()


def per_device(n_leaf, leaf_basis, transfer, transfer_top, coupling_parts, row_slot, col_node):
    any_ = pl.BlockSpec(memory_space=pl.ANY)
    smem = pl.BlockSpec(memory_space=pltpu.SMEM)
    shape = jax.ShapeDtypeStruct
    dma = pltpu.SemaphoreType.DMA
    results = [
        shape((4, PTS, N), BF16),
        shape((7, N, N), F32),
        shape((2, 32, N), F32),
        shape((1, 32, N), F32),
        shape((16, N, N), BF16),
    ]
    outs = pl.pallas_call(
        functools.partial(main_kernel, n_leaf),
        out_shape=[pltpu.VMEM(r.shape, r.dtype) for r in results],
        in_specs=[smem] * 2 + [any_] * 4,
        out_specs=[any_] * 5,
        scratch_shapes=[
            pltpu.VMEM((4, PTS, N), BF16),
            pltpu.VMEM((7, N, N), F32),
            pltpu.VMEM((2, N, N), F32),
            pltpu.VMEM((7, N, N), F32),
            pltpu.VMEM((3, N, N), F32),
            pltpu.VMEM((4, N, N), F32),
            pltpu.VMEM((2, 8, N, N), BF16),
            pltpu.VMEM((2, 16, N, N), BF16),
            pltpu.VMEM((16, N, N), BF16),
            pltpu.VMEM((2, 8, N, N), BF16),
            pltpu.VMEM((7, N, N), BF16),
            pltpu.VMEM((5, 32, 16, N), BF16),
            pltpu.VMEM((4, PTS, N), BF16),
            pltpu.VMEM((7, N, N), F32),
            pltpu.VMEM((2, 32, N), F32),
            pltpu.VMEM((1, 32, N), F32),
            pltpu.VMEM((16, N, N), BF16),
            pltpu.VMEM((16, N, N), BF16),
            dma((6,)), dma((8,)), dma((8,)), dma((2,)), dma((2,)), dma((4,)), dma((4,)), dma((7,)),
            pltpu.SemaphoreType.REGULAR,
        ],
        compiler_params=pltpu.CompilerParams(
            collective_id=0, has_side_effects=True, vmem_limit_bytes=MAIN_VMEM
        ),
        name="factor_and_send",
    )(row_slot, col_node, leaf_basis, transfer, transfer_top, coupling_parts)
    return pl.pallas_call(
        last_kernel,
        out_shape=results,
        in_specs=[any_] * 5,
        out_specs=[any_] * 5,
        scratch_shapes=[dma((5,))],
        compiler_params=pltpu.CompilerParams(vmem_limit_bytes=LAST_VMEM),
        name="hand_over",
    )(*outs)


def solution(mesh):
    lead = P(("leaf", "dom", "rep"), None, None)
    share = P(("leaf", "dom"), "rep", None)
    return jax.shard_map(
        functools.partial(per_device, mesh.shape["leaf"]),
        mesh=mesh,
        in_specs=(
            lead,
            lead,
            P(("leaf", "dom"), None, None),
            P("rep", ("leaf", "dom"), None, None),
            P(("leaf", "dom", "rep")),
            P(("leaf", "dom", "rep")),
        ),
        out_specs=(lead, lead, share, share, lead),
        check_vma=False,
    )
```
